32 devices in a mesh: seq: 8 (over z, x), head: 4 (over y, core).
Axes of the slice: x: 2, y: 2, z: 4, core: 2. Of those that a mesh axis runs over, the one named last changes fastest.
Arguments:
- hidden: bfloat16 [8, 768, 2560], P('seq', 'head'), may hold values from -6 to 6
- norm_gain: float32 [2560], replicated, may hold values from 0.1 to 1.9
- w_qkv: bfloat16 [2560, 3840], P('seq'), may hold values from -0.15625 to 0.15625
- w_out: bfloat16 [2560, 2560], P(None, 'seq'), may hold values from -0.625 to 0.625
- kv_cache: bfloat16 [8, 4096, 1280], P('seq', None, 'head'), as said below
- new_len: int32 [8], replicated, may hold values from 1 to 768, 3072 in all
- prefix_len: int32 [8], replicated, may hold values from 0 to 12287
Outputs:
- attn_out: bfloat16 [8, 768, 2560], P('seq', 'head')
- kv_written: bfloat16 [8, 768, 1280], P('seq', None, 'head')
The draws below stay inside these ranges and needn't reach their ends.
Inputs may be any that keep to these rules, and one draw needn't show every extreme that they name: `new_len`: the lengths sum to 3072 and the largest is 768. `kv_cache`: keys are stored already rotated to their positions.
All inputs are finite; a program needn't handle non-finite values.
Results may differ from the reference program's by a relative error of at most 0.008.
The reference program's roundings to bfloat16 on the way (of `normed`, `probabilities` and `attended`) count: a program that leaves them out, or rounds other values in their place, can miss the bound.
Values may be sent and summed in bfloat16 or wider, within the bound.
No kernel may reach another device: no remote copies, remote signals or barrier semaphores. Data moves between devices by JAX's collectives and lax.ppermute only.
A program may use at most 128 MiB of HBM per device.

```python
import math
import jax
import jax.numpy as jnp
import numpy as np
from jax import lax

D = 2560
Q_HEADS = 32
KV_HEADS = 8
HEAD_DIM = 80
WINDOW = 4096
GROUP = 4
REQS = 8
NEW_REQ = 768


def draw_kv_cache(key, part):
    columns = 2 * KV_HEADS * HEAD_DIM
    drawn = 1.4 * jnp.clip(jax.random.normal(key, (REQS, WINDOW, columns), jnp.float32), -6.0, 6.0)
    return drawn.astype(jnp.bfloat16)


def with_ends(values, stream_key, least, largest):
    shape = values.shape
    place = [jax.random.randint(jax.random.fold_in(stream_key, axis), (), 0, shape[axis]) for axis in range(len(shape))]
    values = values.at[tuple(place)].set(least)
    longest = shape.index(max(shape))
    place[longest] = (place[longest] + 1) % shape[longest]
    return values.at[tuple(place)].set(largest)


def shard_levels(stream_key, extent, pieces, smallest, largest):
    level, own = 1.0, jax.random.fold_in(stream_key, 6)
    for dim, shards_of in pieces:
        heights = jnp.exp(jax.random.uniform(jax.random.fold_in(own, dim), (shards_of,), jnp.float32, smallest / len(pieces), largest / len(pieces)))
        level = level * jnp.repeat(heights, extent[dim] // shards_of).reshape([-1 if axis == dim else 1 for axis in range(len(extent))])
    return level


def profile(count, total, reach, skew):
    weights = [(1 << 20) // math.isqrt(grade ** skew) + 1 for grade in range(2, count + 1)]
    spare, given = total - reach - (count - 1), [1] * (count - 1)
    while spare > 0:
        candidates = [i for i in range(count - 1) if given[i] < reach]
        whole, budget = sum([weights[i] for i in candidates]), spare
        for i in candidates:
            addition = min(reach - given[i], max(1, budget * weights[i] // whole), spare)
            given[i] = given[i] + addition
            spare = spare - addition
    return np.array([reach] + given)


def ragged(stream_key, number_of, total, reach, slope):
    if number_of == 2:
        one = jax.random.randint(stream_key, (), max(1, total - reach), min(reach, total - 1) + 1)
        return jnp.stack([one, total - one])
    sizes = jnp.asarray(profile(number_of, total, reach, slope), jnp.int32)
    pairs = (number_of - 1) // 2
    giver, sink = sizes[1:1 + 2 * pairs:2], sizes[2:2 + 2 * pairs:2]
    margin = jnp.minimum(giver - 1, reach - sink)
    shifted = jax.random.randint(jax.random.fold_in(stream_key, 1), (pairs,), 0, 1 << 20) % (margin + 1)
    sizes = sizes.at[1:1 + 2 * pairs:2].set(giver - shifted).at[2:2 + 2 * pairs:2].set(sink + shifted)
    return sizes[jax.random.permutation(jax.random.fold_in(stream_key, 2), number_of)]


def normal_values(own_key, dims, deviation, limit, shards=(), kind=jnp.bfloat16):
    array = jax.random.normal(own_key, dims, jnp.float32) * deviation
    if len(shards) > 0:
        array = shard_levels(own_key, dims, shards, -0.22, 0.18) * array
    return jnp.clip(array, min=-limit, max=limit).astype(kind)


def setup_inputs(seed: int = 0) -> dict:
    arg_keys = jax.random.split(jax.random.key(seed), 8)
    hidden = normal_values(arg_keys[0], (REQS, NEW_REQ, D), 1.0, 6.0, ((0, 8), (1, 4)))
    norm_gain = jnp.clip(1.0 + 0.18 * jax.random.normal(arg_keys[1], (D,), jnp.float32), 0.1, 1.9)
    w_qkv = normal_values(arg_keys[2], (D, KV_HEADS * (GROUP + 2) * HEAD_DIM), (D // 2) ** -0.5, 0.15625, ((0, 8),))
    w_out = normal_values(arg_keys[3], (Q_HEADS * HEAD_DIM, D), (Q_HEADS * HEAD_DIM // 32) ** -0.5, 0.625, ((1, 8),))
    kv_cache = draw_kv_cache(jax.random.fold_in(arg_keys[7], 71), 0)
    new_len = ragged(arg_keys[5], REQS, REQS * NEW_REQ // 2, NEW_REQ, 2).astype(jnp.int32)
    prefix_len = with_ends(jax.random.randint(arg_keys[6], (REQS,), 0, 3 * WINDOW), jax.random.fold_in(arg_keys[6], 1), 0, (3 * WINDOW) - 1).astype(jnp.int32)
    return dict(hidden=hidden, norm_gain=norm_gain, w_qkv=w_qkv, w_out=w_out, kv_cache=kv_cache, new_len=new_len, prefix_len=prefix_len)


def normalize(hidden, norm_gain):
    values = hidden.astype(jnp.float32)
    meansq = lax.optimization_barrier(jnp.mean(values * values, axis=-1, keepdims=True))
    return (values * lax.rsqrt(meansq + 1e-05) * norm_gain).astype(jnp.bfloat16)

def rotate(values, position):
    halfway = values.shape[-1] // 2
    frequency = jnp.exp(jnp.arange(halfway, dtype=jnp.float32) * (-2.0 * math.log(10000.0) / values.shape[-1]))
    angles = position.astype(jnp.float32)[..., None] * frequency
    cosine = jnp.cos(angles)
    sine_part = jnp.sin(angles)
    leading = values[..., :halfway]
    trailing = values[..., halfway:]
    return jnp.concatenate([leading * cosine - trailing * sine_part, trailing * cosine + leading * sine_part], axis=-1)

def reference(hidden, norm_gain, w_qkv, w_out, kv_cache, new_len, prefix_len):
    score_scale = 1.0 / math.sqrt(HEAD_DIM)

    def one_request(request_items):
        tokens, length, prefix, cache_rows = request_items
        normed = normalize(tokens, norm_gain)
        projected = jnp.dot(normed, w_qkv, preferred_element_type=jnp.float32)
        projected = projected.reshape(NEW_REQ, KV_HEADS, GROUP + 2, HEAD_DIM)
        new_index = jnp.arange(NEW_REQ, dtype=jnp.int32)
        position = prefix + new_index
        queries = rotate(projected[:, :, :GROUP], position[:, None, None]).astype(jnp.bfloat16)
        keys_new = rotate(projected[:, :, GROUP], position[:, None]).astype(jnp.bfloat16)
        values_new = projected[:, :, GROUP + 1].astype(jnp.bfloat16)
        live_rows = new_index < length
        written = jnp.stack([keys_new, values_new], axis=2)
        written = jnp.where(live_rows[:, None, None, None], written, jnp.zeros_like(written))
        written = written.reshape(NEW_REQ, KV_HEADS * 2 * HEAD_DIM)
        cached = cache_rows.reshape(WINDOW, KV_HEADS, 2, HEAD_DIM)
        keys_all = jnp.concatenate([cached[:, :, 0], keys_new], axis=0)
        values_all = jnp.concatenate([cached[:, :, 1], values_new], axis=0)
        key_slot = jnp.arange(WINDOW + NEW_REQ, dtype=jnp.int32)
        allowed = (key_slot[None, :] > new_index[:, None]) & (key_slot[None, :] <= new_index[:, None] + WINDOW) & (key_slot[None, :] >= WINDOW - prefix)

        def one_head(head_items):
            head_queries, head_keys, head_values = head_items
            scores = jnp.einsum('qgd,kd->gqk', head_queries.astype(jnp.float32), head_keys.astype(jnp.float32)) * score_scale
            scores = jnp.where(allowed[None], scores, -jnp.inf)
            row_max = lax.optimization_barrier(jnp.max(scores, axis=-1, keepdims=True))
            weights = jnp.exp(scores - row_max)
            probabilities = (weights / lax.optimization_barrier(jnp.sum(weights, axis=-1, keepdims=True))).astype(jnp.bfloat16)
            return jnp.einsum('gqk,kd->qgd', probabilities.astype(jnp.float32), head_values.astype(jnp.float32))
        attended = lax.map(one_head, (jnp.transpose(queries, (1, 0, 2, 3)), jnp.transpose(keys_all, (1, 0, 2)), jnp.transpose(values_all, (1, 0, 2))))
        attended = jnp.transpose(attended, (1, 0, 2, 3))
        attended = jnp.where(live_rows[:, None, None, None], attended, 0.0).astype(jnp.bfloat16)
        attended = attended.reshape(NEW_REQ, Q_HEADS * HEAD_DIM)
        output = jnp.dot(attended, w_out, preferred_element_type=jnp.float32).astype(jnp.bfloat16)
        return (output, written)
    attn_out, kv_written = lax.map(one_request, (hidden, new_len, prefix_len, kv_cache))
    return (attn_out, kv_written)
```

```python
import functools
import math

import jax
import jax.numpy as jnp
import numpy as np
from jax import lax
from jax.experimental import pallas as pl
from jax.experimental.pallas import tpu as pltpu
from jax.sharding import PartitionSpec as P

HEAD_DIM = 80
WINDOW = 4096
GROUP = 4
LANES = 128
KEY_TILE = 1024
CACHE_TILE = 512
SCORE_SCALE = 1.0 / math.sqrt(HEAD_DIM)
LOG2E = math.log2(math.e)
VMEM_LIMIT = 56 * 1024 * 1024
GROUP_OUT = (GROUP * HEAD_DIM + LANES - 1) // LANES * LANES
WHOLE = pl.BlockSpec(memory_space=pltpu.VMEM)
ANYWHERE = pl.BlockSpec(memory_space=pl.ANY)


def ring_order(count):
    return list(range(0, count, 2)) + list(range(count - 1, 0, -2))


def ring_pairs(count):
    order = ring_order(count)
    ahead = [(order[i], order[(i + 1) % count]) for i in range(count)]
    return ahead, [(b, a) for a, b in ahead]


def ring_starts(count, rows):
    order = ring_order(count)
    place = {owner: i for i, owner in enumerate(order)}
    table = []
    for mine in range(count):
        starts = [mine * rows]
        for step in range(1, count // 2):
            starts.append(order[(place[mine] - step) % count] * rows)
            starts.append(order[(place[mine] + step) % count] * rows)
        opposite = order[(place[mine] + count // 2) % count] * rows
        table.append(starts + [opposite, opposite + rows // 2])
    return np.array(table, np.int32)


def ring_steps(block, count):
    ahead, back = ring_pairs(count)
    f = b = block
    for _ in range(1, count // 2):
        f = lax.ppermute(f, "seq", ahead)
        b = lax.ppermute(b, "seq", back)
        yield f, b
    half = block.shape[0] // 2
    yield lax.ppermute(f[:half], "seq", ahead), lax.ppermute(b[half:], "seq", back)


def kernel_call(body, name, flops=0, moved=0, **kwargs):
    return pl.pallas_call(
        body,
        compiler_params=pltpu.CompilerParams(vmem_limit_bytes=VMEM_LIMIT),
        cost_estimate=pl.CostEstimate(flops=flops, bytes_accessed=moved, transcendentals=0),
        name=name,
        **kwargs,
    )


def normalize_kernel(count, *refs):
    chunks, gain_ref, out_ref = refs[:count], refs[count], refs[count + 1]
    for j in range(count):
        rows = chunks[j].shape[0]
        values = chunks[j][...].astype(jnp.float32)
        meansq = jnp.mean(values * values, axis=-1, keepdims=True)
        scaled = values * lax.rsqrt(meansq + 1e-05) * gain_ref[...]
        out_ref[j * rows : (j + 1) * rows, :] = scaled.astype(jnp.bfloat16)


def normalize_all(chunks, gain):
    rows, width = chunks[0].shape
    return kernel_call(
        functools.partial(normalize_kernel, len(chunks)),
        "normalize",
        moved=4 * rows * len(chunks) * width,
        out_shape=jax.ShapeDtypeStruct((rows * len(chunks), width), jnp.bfloat16),
    )(*chunks, gain.reshape(1, width))


def window_at(wide, start):
    base = start // LANES * LANES
    if start + HEAD_DIM <= base + LANES:
        view = wide[:, base : base + LANES]
        return view if start == base else pltpu.roll(view, LANES - (start - base), 1)
    view = wide[:, base : base + 2 * LANES]
    return pltpu.roll(view, view.shape[1] - (start - base), 1)[:, :LANES]


def widen(values):
    rows, width = values.shape
    padded = (width + LANES - 1) // LANES * LANES
    if padded == width:
        return values
    return jnp.concatenate([values, jnp.zeros((rows, padded - width), values.dtype)], axis=1)


def with_ones(values, lane):
    return jnp.where(lane < HEAD_DIM, values, (lane == HEAD_DIM).astype(jnp.float32))


def cache_kernel(groups, cache_ref, *out_refs):
    wide = widen(cache_ref[...].astype(jnp.float32))
    lane = lax.broadcasted_iota(jnp.int32, (1, LANES), 1)
    for g in range(groups):
        keys = window_at(wide, 2 * g * HEAD_DIM)
        values = window_at(wide, (2 * g + 1) * HEAD_DIM)
        out_refs[2 * g][...] = jnp.where(lane < HEAD_DIM, keys, 0.0).astype(jnp.bfloat16)
        out_refs[2 * g + 1][...] = with_ones(values, lane).astype(jnp.bfloat16)


def cached_layout(kv_cache, new_total, groups):
    columns = kv_cache.shape[-1]
    made = kernel_call(
        functools.partial(cache_kernel, groups),
        "cache",
        moved=WINDOW * (2 * columns + 4 * groups * LANES),
        grid=(WINDOW // CACHE_TILE,),
        in_specs=[pl.BlockSpec((CACHE_TILE, columns), lambda i: (i, 0))],
        out_specs=[pl.BlockSpec((CACHE_TILE, LANES), lambda i: (i, 0))] * (2 * groups),
        out_shape=[jax.ShapeDtypeStruct((WINDOW + new_total, LANES), jnp.bfloat16)] * (2 * groups),
    )(kv_cache.reshape(WINDOW, columns))
    return [(made[2 * g], made[2 * g + 1]) for g in range(groups)]


def project_kernel(pieces, first_piece, chunks, scalars, *refs):
    normed_ref, cos_ref, sin_ref = refs[:3]
    parts = refs[3 : 3 + pieces]
    query_ref, keys_out, values_out = refs[5 + pieces : 8 + pieces]
    weight, key_stage, value_stage, part_sems, out_sems = refs[8 + pieces :]
    copies = []
    for i in range(pieces):
        rows = parts[i].shape[0]
        place = pl.multiple_of(scalars[first_piece + i], 16)
        copies.append(
            pltpu.make_async_copy(parts[i], weight.at[pl.ds(place, rows), :], part_sems.at[i])
        )
        copies[-1].start()
    for copy in copies:
        copy.wait()
    lane = lax.broadcasted_iota(jnp.int32, (1, LANES), 1)
    projected = widen(jnp.dot(normed_ref[...], weight[...], preferred_element_type=jnp.float32))
    cosine, sine = cos_ref[...], sin_ref[...]
    for i in range(GROUP + 1):
        head = window_at(projected, i * HEAD_DIM)
        swapped = jnp.where(
            lane < HEAD_DIM // 2,
            pltpu.roll(head, LANES - HEAD_DIM // 2, 1),
            pltpu.roll(head, HEAD_DIM // 2, 1),
        )
        head = (head * cosine + swapped * sine).astype(jnp.bfloat16)
        if i == GROUP:
            key_stage[...] = head
        else:
            query_ref[i] = head
    values = window_at(projected, (GROUP + 1) * HEAD_DIM)
    value_stage[...] = with_ones(values, lane).astype(jnp.bfloat16)
    chunk = normed_ref.shape[0] // chunks
    copies = []
    for j in range(chunks):
        place = pl.multiple_of(WINDOW + scalars[2 + j], 16)
        for k, (stage, out) in enumerate(((key_stage, keys_out), (value_stage, values_out))):
            copies.append(
                pltpu.make_async_copy(
                    stage.at[pl.ds(j * chunk, chunk), :],
                    out.at[pl.ds(place, chunk), :],
                    out_sems.at[2 * j + k],
                )
            )
            copies[-1].start()
    for copy in copies:
        copy.wait()


def project(scalars, first_piece, normed, cosine, sine, pieces, chunks, keys, values):
    total, width = normed.shape
    columns = pieces[0].shape[1]
    count = len(pieces)
    return kernel_call(
        functools.partial(project_kernel, count, first_piece, chunks),
        "project",
        flops=2 * total * width * columns,
        moved=2 * width * (total + columns),
        grid_spec=pltpu.PrefetchScalarGridSpec(
            num_scalar_prefetch=1,
            grid=(),
            in_specs=[WHOLE] * 3 + [ANYWHERE] * (count + 2),
            out_specs=[WHOLE, ANYWHERE, ANYWHERE],
            scratch_shapes=[
                pltpu.VMEM((width, columns), jnp.bfloat16),
                pltpu.VMEM((total, LANES), jnp.bfloat16),
                pltpu.VMEM((total, LANES), jnp.bfloat16),
                pltpu.SemaphoreType.DMA((count,)),
                pltpu.SemaphoreType.DMA((chunks * 2,)),
            ],
        ),
        out_shape=[
            jax.ShapeDtypeStruct((GROUP, total, LANES), jnp.bfloat16),
            jax.ShapeDtypeStruct(keys.shape, jnp.bfloat16),
            jax.ShapeDtypeStruct(values.shape, jnp.bfloat16),
        ],
        input_output_aliases={4 + count: 1, 5 + count: 2},
    )(scalars, normed, cosine, sine, *pieces, keys, values)


def attend_kernel(extras, offset, begin_chunk, count, scalars, *refs):
    query_ref, key_ref, value_ref = refs[:3]
    out_ref = refs[3 + extras]
    length, prefix = scalars[0], scalars[1]
    chunk = query_ref.shape[1] // count
    rows = GROUP * chunk
    oldest = WINDOW - prefix
    lane = lax.broadcasted_iota(jnp.int32, (1, LANES), 1)
    factor = SCORE_SCALE * LOG2E

    def one_chunk(j, unused):
        first = pl.multiple_of(scalars[2 + begin_chunk + j], 16)
        here = pl.ds(pl.multiple_of(j * chunk, 16), chunk)

        @pl.when(first >= length)
        def _():
            out_ref[here, :] = jnp.zeros((chunk, GROUP_OUT), jnp.bfloat16)

        @pl.when(first < length)
        def _():
            query = query_ref[:, here, :].reshape(rows, LANES)
            token = lax.broadcasted_iota(jnp.int32, (GROUP, chunk, 1), 1).reshape(rows, 1) + first

            def scores_of(start, size):
                return lax.dot_general(
                    query,
                    key_ref[pl.ds(start, size), :],
                    (((1,), (1,)), ((), ())),
                    preferred_element_type=jnp.float32,
                )

            def masked(scores, start, size):
                slot = lax.broadcasted_iota(jnp.int32, (1, size), 1) + start
                seen = (slot > token) & (slot <= token + WINDOW) & (slot >= oldest)
                return jnp.where(seen, scores, -jnp.inf)

            def fold(scores, start, size, carry):
                top, total = carry
                new_top = jnp.maximum(top, jnp.max(scores, axis=1, keepdims=True))
                weights = jnp.exp2((scores - new_top) * factor).astype(jnp.bfloat16)
                shrink = jnp.exp2((top - new_top) * factor)
                values = value_ref[pl.ds(start, size), :]
                added = jnp.dot(weights, values, preferred_element_type=jnp.float32)
                return new_top, total * shrink + added

            def finish(total):
                result = total / total[:, HEAD_DIM : HEAD_DIM + 1]
                result = jnp.where((token < length) & (lane < HEAD_DIM), result, 0.0)
                result = result.reshape(GROUP, chunk, LANES)
                columns = [None] * (GROUP_OUT // LANES + 1)
                for i in range(GROUP):
                    start = offset + i * HEAD_DIM
                    base, shift = start // LANES, start % LANES
                    pair = jnp.concatenate(
                        [result[i], jnp.zeros((chunk, LANES), jnp.float32)], axis=1
                    )
                    if shift:
                        pair = pltpu.roll(pair, shift, 1)
                    for k in range(2):
                        piece = pair[:, k * LANES : (k + 1) * LANES]
                        old = columns[base + k]
                        columns[base + k] = piece if old is None else old + piece
                wide = jnp.concatenate(columns[: GROUP_OUT // LANES], axis=1)
                out_ref[here, :] = wide.astype(jnp.bfloat16)

            def at(i):
                return pl.multiple_of(first + i * KEY_TILE, 16)

            newest = at(WINDOW // KEY_TILE)
            none = (
                jnp.full((rows, 1), -1e38, jnp.float32),
                jnp.zeros((rows, LANES), jnp.float32),
            )
            begin = jnp.clip((oldest - first) // KEY_TILE, 0, WINDOW // KEY_TILE - 1)

            @pl.when(begin == 0)
            def _():
                scores = masked(scores_of(newest, chunk), newest, chunk)
                start, size, carry = newest, chunk, none
                for i in range(WINDOW // KEY_TILE):
                    coming = scores_of(at(i), KEY_TILE)
                    if i == 0:
                        coming = masked(coming, at(0), KEY_TILE)
                    carry = fold(scores, start, size, carry)
                    scores, start, size = coming, at(i), KEY_TILE
                finish(fold(scores, start, size, carry)[1])

            @pl.when(begin > 0)
            def _():
                carry = fold(masked(scores_of(newest, chunk), newest, chunk), newest, chunk, none)
                carry = fold(
                    masked(scores_of(at(begin), KEY_TILE), at(begin), KEY_TILE), at(begin), KEY_TILE, carry
                )

                def step(i, c):
                    return fold(scores_of(at(i), KEY_TILE), at(i), KEY_TILE, c)

                finish(lax.fori_loop(begin + 1, WINDOW // KEY_TILE, step, carry)[1])

        return unused

    lax.fori_loop(0, count, one_chunk, 0)


def attend(scalars, query, keys, values, half, chunks, offset, extras=()):
    total = query.shape[1]
    count = chunks // 2
    rows = total // 2
    work = GROUP * rows * (WINDOW + rows // count)
    return kernel_call(
        functools.partial(attend_kernel, len(extras), offset, half * count, count),
        "attend",
        flops=work * 4 * LANES,
        moved=4 * keys.shape[0] * LANES,
        grid_spec=pltpu.PrefetchScalarGridSpec(
            num_scalar_prefetch=1,
            grid=(1,),
            in_specs=[
                pl.BlockSpec((GROUP, rows, LANES), lambda i, s: (0, half, 0)),
                WHOLE,
                WHOLE,
            ]
            + [ANYWHERE] * len(extras),
            out_specs=pl.BlockSpec((rows, GROUP_OUT), lambda i, s: (0, 0)),
        ),
        out_shape=jax.ShapeDtypeStruct((rows, GROUP_OUT), jnp.bfloat16),
    )(scalars, query, keys, values, *extras)


def output_kernel(groups, pieces, first_piece, scalars, *refs):
    attended = refs[:groups]
    parts = refs[groups : groups + pieces]
    out_refs = refs[groups + pieces : -2]
    weight, sems = refs[-2:]
    copies = []
    for i in range(pieces):
        rows = parts[i].shape[0]
        place = pl.multiple_of(scalars[first_piece + i], 16)
        copies.append(pltpu.make_async_copy(parts[i], weight.at[pl.ds(place, rows), :], sems.at[i]))
        copies[-1].start()
    for copy in copies:
        copy.wait()
    depth = weight.shape[1]
    columns = [None] * (depth // LANES + 1)
    for g in range(groups):
        base = g * GROUP * HEAD_DIM // LANES
        for k in range(GROUP_OUT // LANES):
            piece = attended[g][:, k * LANES : (k + 1) * LANES]
            old = columns[base + k]
            columns[base + k] = piece if old is None else old + piece
    used = (depth + LANES - 1) // LANES
    left = jnp.concatenate(columns[:used], axis=1)[:, :depth]
    product = lax.dot_general(
        left, weight[...], (((1,), (1,)), ((), ())), preferred_element_type=jnp.float32
    )
    row = 0
    for out in out_refs:
        out[...] = product[row : row + out.shape[0], :].astype(out.dtype)
        row += out.shape[0]


def output_products(scalars, first_piece, attended, pieces, outs):
    count = len(pieces)
    rows = attended[0].shape[0]
    depth = pieces[0].shape[1]
    width = scalars_width = sum(p.shape[0] for p in pieces)
    return kernel_call(
        functools.partial(output_kernel, len(attended), count, first_piece),
        "output",
        flops=2 * rows * width * depth,
        moved=2 * width * (rows + depth),
        grid_spec=pltpu.PrefetchScalarGridSpec(
            num_scalar_prefetch=1,
            grid=(),
            in_specs=[WHOLE] * len(attended) + [ANYWHERE] * count,
            out_specs=[WHOLE] * len(outs),
            scratch_shapes=[
                pltpu.VMEM((width, depth), jnp.bfloat16),
                pltpu.SemaphoreType.DMA((count,)),
            ],
        ),
        out_shape=[jax.ShapeDtypeStruct((r, width), kind) for r, kind in outs],
    )(scalars, *attended, *pieces)


def rotation_tables(position):
    halfway = HEAD_DIM // 2
    frequency = jnp.exp(
        jnp.arange(halfway, dtype=jnp.float32) * (-2.0 * math.log(10000.0) / HEAD_DIM)
    )
    angles = position.astype(jnp.float32)[..., None] * frequency
    cosine, sine = jnp.cos(angles), jnp.sin(angles)
    rest = jnp.zeros((position.shape[0], LANES - HEAD_DIM), jnp.float32)
    return (
        jnp.concatenate([cosine, cosine, rest], axis=1),
        jnp.concatenate([-sine, sine, rest], axis=1),
    )


def shards(hidden, norm_gain, w_qkv, w_out, kv_cache, new_len, prefix_len):
    seq_index = lax.axis_index("seq")
    head_index = lax.axis_index("head")
    seq_count = lax.axis_size("seq")
    head_count = lax.axis_size("head")
    unused_lead, chunk, width = hidden.shape
    depth, total_cols = w_qkv.shape
    groups = total_cols // ((GROUP + 2) * HEAD_DIM) // head_count
    group_width = (GROUP + 2) * HEAD_DIM
    head_cols = groups * GROUP * HEAD_DIM
    out_depth = w_out.shape[1]
    new_total = head_count * chunk
    paired = head_count == 4
    core_pairs = [(i, i ^ 1) for i in range(head_count)]
    y_pairs = [(i, i ^ 2) for i in range(head_count)]

    if paired:
        order = np.array([[h ^ j for j in range(head_count)] for h in range(head_count)])
    else:
        order = np.array([[(h + j) % head_count for j in range(head_count)] for h in range(head_count)])
    ring_table = np.concatenate([ring_starts(seq_count, depth), ring_starts(seq_count, out_depth)], axis=1)
    chunk_rows = jnp.asarray((order * chunk).astype(np.int32))[head_index]
    scalars = jnp.concatenate(
        [new_len[seq_index][None], prefix_len[seq_index][None], chunk_rows, jnp.asarray(ring_table)[seq_index]]
    )
    first_qkv = 2 + head_count
    first_out = first_qkv + seq_count + 1
    length, prefix = scalars[0], scalars[1]

    starts = [
        lax.dynamic_slice_in_dim(w_qkv, (head_index * groups + g) * group_width, group_width, 1)
        for g in range(groups)
    ]
    pieces = [[s] for s in starts]
    for step in zip(*[ring_steps(s, seq_count) for s in starts]):
        for g, arrived in enumerate(step):
            pieces[g].extend(arrived)

    own_hidden = hidden.reshape(chunk, width)
    if paired:
        far = lax.ppermute(own_hidden, "head", y_pairs)
        near = lax.ppermute(own_hidden, "head", core_pairs)
        chunks = [own_hidden, near, far, lax.ppermute(far, "head", core_pairs)]
    else:
        gathered = lax.all_gather(own_hidden, "head", axis=0)
        chunks = [
            lax.dynamic_index_in_dim(gathered, (head_index + j) % head_count, 0, keepdims=False)
            for j in range(head_count)
        ]
    normed = normalize_all(chunks, norm_gain)
    token = (chunk_rows[:, None] + jnp.arange(chunk, dtype=jnp.int32)).reshape(new_total)
    cosine, sine = rotation_tables(prefix + token)
    cached = cached_layout(kv_cache, new_total, groups)

    out_rows = lax.dynamic_slice_in_dim(w_out, head_index * head_cols, head_cols, 0).T
    out_rows, _ = lax.optimization_barrier((out_rows, pieces[0][-1]))
    out_pieces = [out_rows]
    out_steps = []
    for arrived in ring_steps(out_rows, seq_count):
        out_pieces.extend(arrived)
        out_steps.append(arrived)

    attended = [[None] * groups, [None] * groups]
    written = []
    for g in range(groups):
        query, keys, values = project(
            scalars, first_qkv, normed, cosine, sine, pieces[g], head_count, *cached[g]
        )
        written += [keys[WINDOW:, :HEAD_DIM], values[WINDOW:, :HEAD_DIM]]
        offset = g * GROUP * HEAD_DIM % LANES
        for half in (1, 0):
            attended[half][g] = attend(scalars, query, keys, values, half, head_count, offset)
    live_rows = jnp.arange(new_total, dtype=jnp.int32) < length
    written = jnp.concatenate(written, axis=1)
    written = jnp.where(live_rows[:, None], written, jnp.zeros_like(written))
    kv_written = written.reshape(1, new_total, groups * 2 * HEAD_DIM)

    if paired:
        forth, across = output_products(
            scalars, first_out, attended[1], out_pieces, [(chunk, jnp.bfloat16)] * 2
        )
        beside = lax.ppermute(across, "head", core_pairs)
        both = (forth.astype(jnp.float32) + beside.astype(jnp.float32)).astype(jnp.bfloat16)
        far = lax.ppermute(both, "head", y_pairs)
        own, other = output_products(
            scalars, first_out, attended[0], out_pieces, [(chunk, jnp.float32), (chunk, jnp.bfloat16)]
        )
        near = lax.ppermute(other, "head", core_pairs)
        output = own + near.astype(jnp.float32) + far.astype(jnp.float32)
    else:
        products = [
            output_products(scalars, first_out, part, out_pieces, [(new_total // 2, jnp.bfloat16)])[0]
            for part in attended
        ]
        stacked = jnp.concatenate(products, axis=0).reshape(head_count, chunk, width)
        back = jnp.asarray((np.arange(head_count)[None] - np.arange(head_count)[:, None]) % head_count)
        output = lax.psum_scatter(stacked[back[head_index]], "head", scatter_dimension=0)
    return (output.astype(jnp.bfloat16).reshape(1, chunk, width), kv_written)


def solution(mesh):
    placed = (
        P("seq", "head", None),
        P(),
        P("seq", None),
        P(None, "seq"),
        P("seq", None, "head"),
        P(),
        P(),
    )
    return jax.shard_map(
        shards,
        mesh=mesh,
        in_specs=placed,
        out_specs=(P("seq", "head", None), P("seq", None, "head")),
        check_vma=False,
    )
```

```python
import functools
import math

import jax
import jax.numpy as jnp
import numpy as np
from jax import lax
from jax.experimental import pallas as pl
from jax.experimental.pallas import tpu as pltpu
from jax.sharding import PartitionSpec as P

HEAD_DIM = 80
WINDOW = 4096
GROUP = 4
LANES = 128
KEY_TILE = 1024
VALUE_ROWS = HEAD_DIM + 16
SCORE_SCALE = 1.0 / math.sqrt(HEAD_DIM)
LOG2E = math.log2(math.e)
FLOPS_PER_US = 1.1e9
GROUP_OUT = (GROUP * HEAD_DIM + LANES - 1) // LANES * LANES
WHOLE = pl.BlockSpec(memory_space=pltpu.VMEM)
ANYWHERE = pl.BlockSpec(memory_space=pl.ANY)


def ring_order(count):
    return list(range(0, count, 2)) + list(range(count - 1, 0, -2))


def ring_pairs(count):
    order = ring_order(count)
    ahead = [(order[i], order[(i + 1) % count]) for i in range(count)]
    return ahead, [(b, a) for a, b in ahead]


def ring_starts(count, rows):
    order = ring_order(count)
    place = {owner: i for i, owner in enumerate(order)}
    table = []
    for mine in range(count):
        starts = [mine * rows]
        for step in range(1, count // 2):
            starts.append(order[(place[mine] - step) % count] * rows)
            starts.append(order[(place[mine] + step) % count] * rows)
        opposite = order[(place[mine] + count // 2) % count] * rows
        table.append(starts + [opposite, opposite + rows // 2])
    return np.array(table, np.int32)


def ring_steps(block, count):
    ahead, back = ring_pairs(count)
    f = b = block
    for _ in range(1, count // 2):
        f = lax.ppermute(f, "seq", ahead)
        b = lax.ppermute(b, "seq", back)
        yield f, b
    half = block.shape[0] // 2
    yield lax.ppermute(f[:half], "seq", ahead), lax.ppermute(b[half:], "seq", back)


def kernel_call(body, name, room, micros, **kwargs):
    return pl.pallas_call(
        body,
        compiler_params=pltpu.CompilerParams(vmem_limit_bytes=room * 1024 * 1024),
        cost_estimate=pl.CostEstimate(flops=int(micros * FLOPS_PER_US), bytes_accessed=0, transcendentals=0),
        name=name,
        **kwargs,
    )


def tie(value, *earlier):
    return lax.optimization_barrier((value, *earlier))[0]


def normalize_kernel(count, first_chunk, scalars, *refs):
    chunks, gain_ref, out_ref = refs[:count], refs[count], refs[-3]
    stage, sems = refs[-2:]
    copies = []
    for j in range(count):
        rows = chunks[j].shape[0]
        values = chunks[j][...].astype(jnp.float32)
        meansq = jnp.mean(values * values, axis=-1, keepdims=True)
        scaled = values * lax.rsqrt(meansq + 1e-05) * gain_ref[...]
        stage[j] = scaled.astype(jnp.bfloat16)
        place = pl.multiple_of(scalars[2 + first_chunk + j], 16)
        copies.append(pltpu.make_async_copy(stage.at[j], out_ref.at[pl.ds(place, rows), :], sems.at[j]))
        copies[-1].start()
    for copy in copies:
        copy.wait()


def normalize_some(scalars, first_chunk, chunks, gain, total, into=None):
    rows, width = chunks[0].shape
    count = len(chunks)
    more = [] if into is None else [into]
    return kernel_call(
        functools.partial(normalize_kernel, count, first_chunk),
        "normalize",
        16,
        3.5,
        grid_spec=pltpu.PrefetchScalarGridSpec(
            num_scalar_prefetch=1,
            grid=(),
            in_specs=[WHOLE] * (count + 1) + [ANYWHERE] * len(more),
            out_specs=ANYWHERE,
            scratch_shapes=[
                pltpu.VMEM((count, rows, width), jnp.bfloat16),
                pltpu.SemaphoreType.DMA((count,)),
            ],
        ),
        out_shape=jax.ShapeDtypeStruct((total, width), jnp.bfloat16),
        input_output_aliases={count + 2: 0} if more else {},
    )(scalars, *chunks, gain.reshape(1, width), *more)


def window_at(wide, start):
    base = start // LANES * LANES
    if start + HEAD_DIM <= base + LANES:
        view = wide[:, base : base + LANES]
        return view if start == base else pltpu.roll(view, LANES - (start - base), 1)
    view = wide[:, base : base + 2 * LANES]
    return pltpu.roll(view, view.shape[1] - (start - base), 1)[:, :LANES]


def widen(values):
    rows, width = values.shape
    padded = (width + LANES - 1) // LANES * LANES
    if padded == width:
        return values
    return jnp.concatenate([values, jnp.zeros((rows, padded - width), values.dtype)], axis=1)


def project_kernel(pieces, first_piece, groups, scalars, *refs):
    normed_ref, cos_ref, sin_ref = refs[:3]
    parts = refs[3 : 3 + pieces]
    query_ref, new_ref, written_ref = refs[3 + pieces : 6 + pieces]
    weight, part_sems = refs[6 + pieces :]
    copies = []
    for i in range(pieces):
        rows = parts[i].shape[0]
        place = pl.multiple_of(scalars[first_piece + i], 16)
        copies.append(
            pltpu.make_async_copy(parts[i], weight.at[pl.ds(place, rows), :], part_sems.at[i])
        )
        copies[-1].start()
    for copy in copies:
        copy.wait()
    lane = lax.broadcasted_iota(jnp.int32, (1, LANES), 1)
    projected = widen(jnp.dot(normed_ref[...], weight[...], preferred_element_type=jnp.float32))
    total = projected.shape[0]
    cosine, sine = cos_ref[...], sin_ref[...]
    live = lax.broadcasted_iota(jnp.int32, (1, total), 1) < scalars[0]
    for g in range(groups):
        for i in range(GROUP + 2):
            head = window_at(projected, (g * (GROUP + 2) + i) * HEAD_DIM)
            if i <= GROUP:
                swapped = jnp.where(
                    lane < HEAD_DIM // 2,
                    pltpu.roll(head, LANES - HEAD_DIM // 2, 1),
                    pltpu.roll(head, HEAD_DIM // 2, 1),
                )
                head = head * cosine + swapped * sine
            if i < GROUP:
                query_ref[g * GROUP + i] = head.astype(jnp.bfloat16)
            else:
                turned = jnp.transpose(head)[:HEAD_DIM, :]
                first = (2 * g + i - GROUP) * HEAD_DIM
                rows = slice(first, first + HEAD_DIM)
                new_ref[rows, :] = turned.astype(jnp.bfloat16)
                written_ref[rows, :] = jnp.where(live, turned, 0.0).astype(jnp.bfloat16)


def project(scalars, first_piece, normed, cosine, sine, pieces):
    total, width = normed.shape
    columns = pieces[0].shape[1]
    groups = columns // ((GROUP + 2) * HEAD_DIM)
    count = len(pieces)
    return kernel_call(
        functools.partial(project_kernel, count, first_piece, groups),
        "project",
        32,
        8,
        grid_spec=pltpu.PrefetchScalarGridSpec(
            num_scalar_prefetch=1,
            grid=(),
            in_specs=[WHOLE] * 3 + [ANYWHERE] * count,
            out_specs=[WHOLE] * 3,
            scratch_shapes=[
                pltpu.VMEM((width, columns), jnp.bfloat16),
                pltpu.SemaphoreType.DMA((count,)),
            ],
        ),
        out_shape=[
            jax.ShapeDtypeStruct((groups * GROUP, total, LANES), jnp.bfloat16),
            jax.ShapeDtypeStruct((groups * 2 * HEAD_DIM, total), jnp.bfloat16),
            jax.ShapeDtypeStruct((groups * 2 * HEAD_DIM, total), jnp.bfloat16),
        ],
    )(scalars, normed, cosine, sine, *pieces)


def attend_kernel(extras, group, begin_chunk, count, chunk, scalars, *refs):
    query_ref, cache_ref, new_ref = refs[:3]
    out_ref = refs[3 + extras]
    keys, values, sems = refs[4 + extras :]
    length, prefix = scalars[0], scalars[1]
    rows = GROUP * chunk
    oldest = WINDOW - prefix
    lane = lax.broadcasted_iota(jnp.int32, (1, VALUE_ROWS), 1)
    factor = SCORE_SCALE * LOG2E
    offset = group * GROUP * HEAD_DIM % LANES
    total_slots = keys.shape[1]
    span = (chunk + LANES - 1) // LANES * LANES
    head_rows = pl.ds(0, HEAD_DIM)
    spans = [(WINDOW, total_slots - WINDOW)] + [(i, KEY_TILE) for i in range(0, WINDOW, KEY_TILE)]
    copies = []
    for n, (start, size) in enumerate(spans):
        for k, room in enumerate((keys, values)):
            if n == 0:
                source = new_ref.at[pl.ds((2 * group + k) * HEAD_DIM, HEAD_DIM), :]
            else:
                source = cache_ref.at[pl.ds((2 * group + k) * HEAD_DIM, HEAD_DIM), pl.ds(start, size)]
            copies.append(
                pltpu.make_async_copy(source, room.at[head_rows, pl.ds(start, size)], sems.at[2 * n + k])
            )
            copies[-1].start()
    ones = lax.broadcasted_iota(jnp.int32, (VALUE_ROWS - HEAD_DIM, total_slots), 0) == 0
    values[HEAD_DIM:, :] = ones.astype(jnp.float32).astype(jnp.bfloat16)
    for copy in copies:
        copy.wait()

    def one_chunk(j, unused):
        first = pl.multiple_of(scalars[2 + begin_chunk + j], 16)
        base = pl.multiple_of(first // LANES * LANES, LANES)
        here = pl.ds(pl.multiple_of(j * chunk, 16), chunk)

        @pl.when(first >= length)
        def _():
            out_ref[here, :] = jnp.zeros((chunk, GROUP_OUT), jnp.bfloat16)

        @pl.when(first < length)
        def _():
            query = query_ref[:, pl.ds(first, chunk), :].reshape(rows, LANES)[:, :HEAD_DIM]
            token = lax.broadcasted_iota(jnp.int32, (GROUP, chunk, 1), 1).reshape(rows, 1) + first

            def scores_of(start, size):
                return jnp.dot(query, keys[:, pl.ds(start, size)], preferred_element_type=jnp.float32)

            ahead_of = lax.broadcasted_iota(jnp.int32, (1, span), 1) - (token - base)

            def recent(scores):
                return jnp.where(ahead_of <= 0, scores, -jnp.inf)

            def oldest_in(scores, start):
                slot = lax.broadcasted_iota(jnp.int32, (1, KEY_TILE), 1) + start
                scores = jnp.where(slot >= oldest, scores, -jnp.inf)
                edge = jnp.where(ahead_of + (start - base) > 0, scores[:, :span], -jnp.inf)
                return jnp.concatenate([edge, scores[:, span:]], axis=1)

            def fold(scores, start, size, carry):
                top, total = carry
                new_top = jnp.maximum(top, jnp.max(scores, axis=1, keepdims=True))
                weights = jnp.exp2((scores - new_top) * factor).astype(jnp.bfloat16)
                shrink = jnp.exp2((top - new_top) * factor)
                added = lax.dot_general(
                    weights,
                    values[:, pl.ds(start, size)],
                    (((1,), (1,)), ((), ())),
                    preferred_element_type=jnp.float32,
                )
                return new_top, total * shrink + added

            def finish(total):
                result = total / total[:, HEAD_DIM : HEAD_DIM + 1]
                result = jnp.where((token < length) & (lane < HEAD_DIM), result, 0.0)
                rest = jnp.zeros((rows, 2 * LANES - VALUE_ROWS), jnp.float32)
                result = jnp.concatenate([result, rest], axis=1).reshape(GROUP, chunk, 2 * LANES)
                columns = [None] * (GROUP_OUT // LANES + 1)
                for i in range(GROUP):
                    start = offset + i * HEAD_DIM
                    base, shift = start // LANES, start % LANES
                    pair = pltpu.roll(result[i], shift, 1) if shift else result[i]
                    for k in range(2):
                        piece = pair[:, k * LANES : (k + 1) * LANES]
                        old = columns[base + k]
                        columns[base + k] = piece if old is None else old + piece
                wide = jnp.concatenate(columns[: GROUP_OUT // LANES], axis=1)
                out_ref[here, :] = wide.astype(jnp.bfloat16)

            def at(i):
                return pl.multiple_of(base + i * KEY_TILE, LANES)

            newest = at(WINDOW // KEY_TILE)
            none = (
                jnp.full((rows, 1), -1e38, jnp.float32),
                jnp.zeros((rows, VALUE_ROWS), jnp.float32),
            )
            begin = jnp.clip((oldest - base) // KEY_TILE, 0, WINDOW // KEY_TILE - 1)

            @pl.when(begin == 0)
            def _():
                scores = recent(scores_of(newest, span))
                start, size, carry = newest, span, none
                for i in range(WINDOW // KEY_TILE):
                    coming = scores_of(at(i), KEY_TILE)
                    if i == 0:
                        coming = oldest_in(coming, at(0))
                    carry = fold(scores, start, size, carry)
                    scores, start, size = coming, at(i), KEY_TILE
                finish(fold(scores, start, size, carry)[1])

            @pl.when(begin > 0)
            def _():
                carry = fold(recent(scores_of(newest, span)), newest, span, none)
                carry = fold(oldest_in(scores_of(at(begin), KEY_TILE), at(begin)), at(begin), KEY_TILE, carry)

                def step(i, c):
                    return fold(scores_of(at(i), KEY_TILE), at(i), KEY_TILE, c)

                finish(lax.fori_loop(begin + 1, WINDOW // KEY_TILE, step, carry)[1])

        return unused

    lax.fori_loop(0, count, one_chunk, 0)


def attend(scalars, query, cache, new, group, half, chunk, extras=()):
    total = query.shape[1]
    rows = total // 2
    count = rows // chunk
    slots = WINDOW + total
    return kernel_call(
        functools.partial(attend_kernel, len(extras), group, half * count, count, chunk),
        "attend",
        32,
        10,
        grid_spec=pltpu.PrefetchScalarGridSpec(
            num_scalar_prefetch=1,
            grid=(1,),
            in_specs=[pl.BlockSpec((GROUP, total, LANES), lambda i, s: (group, 0, 0))]
            + [ANYWHERE] * (2 + len(extras)),
            out_specs=pl.BlockSpec((rows, GROUP_OUT), lambda i, s: (0, 0)),
            scratch_shapes=[
                pltpu.VMEM((HEAD_DIM, slots), jnp.bfloat16),
                pltpu.VMEM((VALUE_ROWS, slots), jnp.bfloat16),
                pltpu.SemaphoreType.DMA((2 * (1 + WINDOW // KEY_TILE),)),
            ],
        ),
        out_shape=jax.ShapeDtypeStruct((rows, GROUP_OUT), jnp.bfloat16),
    )(scalars, query, cache, new, *extras)


def output_kernel(groups, pieces, first_piece, scalars, *refs):
    attended = refs[:groups]
    parts = refs[groups : groups + pieces]
    out_refs = refs[groups + pieces : -2]
    weight, sems = refs[-2:]
    copies = []
    for i in range(pieces):
        rows = parts[i].shape[0]
        place = pl.multiple_of(scalars[first_piece + i], 16)
        copies.append(pltpu.make_async_copy(parts[i], weight.at[pl.ds(place, rows), :], sems.at[i]))
        copies[-1].start()
    for copy in copies:
        copy.wait()
    depth = weight.shape[1]
    columns = [None] * (depth // LANES + 1)
    for g in range(groups):
        base = g * GROUP * HEAD_DIM // LANES
        for k in range(GROUP_OUT // LANES):
            piece = attended[g][:, k * LANES : (k + 1) * LANES]
            old = columns[base + k]
            columns[base + k] = piece if old is None else old + piece
    used = (depth + LANES - 1) // LANES
    left = jnp.concatenate(columns[:used], axis=1)[:, :depth]
    product = lax.dot_general(
        left, weight[...], (((1,), (1,)), ((), ())), preferred_element_type=jnp.float32
    )
    row = 0
    for out in out_refs:
        out[...] = product[row : row + out.shape[0], :].astype(out.dtype)
        row += out.shape[0]


def output_products(scalars, first_piece, attended, pieces, outs):
    count = len(pieces)
    rows = attended[0].shape[0]
    depth = pieces[0].shape[1]
    width = sum(p.shape[0] for p in pieces)
    return kernel_call(
        functools.partial(output_kernel, len(attended), count, first_piece),
        "output",
        28,
        4.5,
        grid_spec=pltpu.PrefetchScalarGridSpec(
            num_scalar_prefetch=1,
            grid=(),
            in_specs=[WHOLE] * len(attended) + [ANYWHERE] * count,
            out_specs=[WHOLE] * len(outs),
            scratch_shapes=[
                pltpu.VMEM((width, depth), jnp.bfloat16),
                pltpu.SemaphoreType.DMA((count,)),
            ],
        ),
        out_shape=[jax.ShapeDtypeStruct((r, width), kind) for r, kind in outs],
    )(scalars, *attended, *pieces)


def rotation_tables(position):
    halfway = HEAD_DIM // 2
    frequency = jnp.exp(
        jnp.arange(halfway, dtype=jnp.float32) * (-2.0 * math.log(10000.0) / HEAD_DIM)
    )
    angles = position.astype(jnp.float32)[..., None] * frequency
    cosine, sine = jnp.cos(angles), jnp.sin(angles)
    rest = jnp.zeros((position.shape[0], LANES - HEAD_DIM), jnp.float32)
    return (
        jnp.concatenate([cosine, cosine, rest], axis=1),
        jnp.concatenate([-sine, sine, rest], axis=1),
    )


def shards(hidden, norm_gain, w_qkv, w_out, kv_cache, new_len, prefix_len):
    seq_index = lax.axis_index("seq")
    head_index = lax.axis_index("head")
    seq_count = lax.axis_size("seq")
    head_count = lax.axis_size("head")
    unused_lead, chunk, width = hidden.shape
    depth, total_cols = w_qkv.shape
    groups = total_cols // ((GROUP + 2) * HEAD_DIM) // head_count
    group_width = (GROUP + 2) * HEAD_DIM
    head_cols = groups * GROUP * HEAD_DIM
    out_depth = w_out.shape[1]
    new_total = head_count * chunk
    paired = head_count == 4
    core_pairs = [(i, i ^ 1) for i in range(head_count)]
    y_pairs = [(i, i ^ 2) for i in range(head_count)]

    if paired:
        order = np.array([[h ^ j for j in range(head_count)] for h in range(head_count)])
    else:
        order = np.array([[(h + j) % head_count for j in range(head_count)] for h in range(head_count)])
    ring_table = np.concatenate([ring_starts(seq_count, depth), ring_starts(seq_count, out_depth)], axis=1)
    chunk_rows = jnp.asarray((order * chunk).astype(np.int32))[head_index]
    scalars = jnp.concatenate(
        [new_len[seq_index][None], prefix_len[seq_index][None], chunk_rows, jnp.asarray(ring_table)[seq_index]]
    )
    first_qkv = 2 + head_count
    first_out = first_qkv + seq_count + 1
    length, prefix = scalars[0], scalars[1]

    own_hidden = hidden.reshape(chunk, width)
    if paired:
        far = lax.ppermute(own_hidden, "head", y_pairs)
        last = lax.ppermute(far, "head", core_pairs)
    else:
        gathered = lax.all_gather(own_hidden, "head", axis=0)
        chunks = [
            lax.dynamic_index_in_dim(gathered, (head_index + j) % head_count, 0, keepdims=False)
            for j in range(head_count)
        ]
        far = last = gathered

    ahead, back = ring_pairs(seq_count)
    own_cols = lax.dynamic_slice_in_dim(
        w_qkv, head_index * groups * group_width, groups * group_width, 1
    )
    pieces = [own_cols]
    f = b = own_cols
    cosine, sine = rotation_tables(prefix + jnp.arange(new_total, dtype=jnp.int32))
    final = seq_count // 2
    for step in range(1, final + 1):
        if step == 2 and paired:
            chunks = [own_hidden, lax.ppermute(tie(own_hidden, f), "head", core_pairs), far, last]
        if step == final:
            normed = normalize_some(scalars, 0, chunks[: head_count // 2], norm_gain, new_total)
            normed = normalize_some(
                scalars, head_count // 2, chunks[head_count // 2 :], norm_gain, new_total, normed
            )
            f, b = f[: depth // 2], b[depth // 2 :]
            f, b = lax.optimization_barrier((f, b, last, cosine, sine))[:2]
        elif step == final - 1:
            f, b = lax.optimization_barrier((f, b, far))[:2]
        elif step > 1:
            f, b = lax.optimization_barrier((f, b))
        full = (f, b)
        f, b = lax.ppermute(f, "seq", ahead), lax.ppermute(b, "seq", back)
        pieces += [f, b]

    cache = kv_cache.reshape(WINDOW, kv_cache.shape[-1]).T

    out_rows = lax.dynamic_slice_in_dim(w_out, head_index * head_cols, head_cols, 0).T
    out_rows = tie(out_rows, *full)
    out_pieces = [out_rows]
    out_steps = []
    for arrived in ring_steps(out_rows, seq_count):
        out_pieces.extend(arrived)
        out_steps.append(arrived)

    attended = [[None] * groups, [None] * groups]
    waits = iter(out_steps if paired else [()] * len(out_steps))
    query, new, written = project(tie(scalars, *next(waits)), first_qkv, normed, cosine, sine, pieces)
    for g in range(groups):
        attended[1][g] = attend(scalars, query, cache, new, g, 1, chunk, next(waits, ()))
    late = scalars
    arrived = []
    for g in range(groups):
        if paired and g == 0:
            forth, across = output_products(
                scalars, first_out, attended[1], out_pieces, [(chunk, jnp.bfloat16)] * 2
            )
            beside = lax.ppermute(across, "head", core_pairs)
            both = (forth.astype(jnp.float32) + beside.astype(jnp.float32)).astype(jnp.bfloat16)
            cut = (width * 9 // 20 + LANES - 1) // LANES * LANES
            parts = [both[:, :cut], both[:, cut : 2 * cut], both[:, 2 * cut :]]
            late = tie(scalars, *parts)
        attended[0][g] = attend(late, query, cache, new, g, 0, chunk)
        if paired:
            arrived.append(lax.ppermute(parts[g], "head", y_pairs))
            late = tie(late, arrived[g], attended[0][g])
    kv_written = written.T.reshape(1, new_total, groups * 2 * HEAD_DIM)

    if paired:
        own, other = output_products(
            late, first_out, attended[0], out_pieces, [(chunk, jnp.float32), (chunk, jnp.bfloat16)]
        )
        arrived += [lax.ppermute(part, "head", y_pairs) for part in parts[groups:]]
        near = lax.ppermute(other, "head", core_pairs)
        far = jnp.concatenate(arrived, axis=1)
        output = own + near.astype(jnp.float32) + far.astype(jnp.float32)
    else:
        products = [
            output_products(scalars, first_out, part, out_pieces, [(new_total // 2, jnp.bfloat16)])[0]
            for part in attended
        ]
        stacked = jnp.concatenate(products, axis=0).reshape(head_count, chunk, width)
        back = jnp.asarray((np.arange(head_count)[None] - np.arange(head_count)[:, None]) % head_count)
        output = lax.psum_scatter(stacked[back[head_index]], "head", scatter_dimension=0)
    return (output.astype(jnp.bfloat16).reshape(1, chunk, width), kv_written)


def solution(mesh):
    placed = (
        P("seq", "head", None),
        P(),
        P("seq", None),
        P(None, "seq"),
        P("seq", None, "head"),
        P(),
        P(),
    )
    return jax.shard_map(
        shards,
        mesh=mesh,
        in_specs=placed,
        out_specs=(P("seq", "head", None), P("seq", None, "head")),
        check_vma=False,
    )
```

```python
import functools
import math

import jax
import jax.numpy as jnp
import numpy as np
from jax import lax
from jax.experimental import pallas as pl
from jax.experimental.pallas import tpu as pltpu
from jax.sharding import PartitionSpec as P

HEAD_DIM = 80
WINDOW = 4096
GROUP = 4
LANES = 128
KEY_TILE = 1024
VALUE_ROWS = HEAD_DIM + 16
SCORE_SCALE = 1.0 / math.sqrt(HEAD_DIM)
LOG2E = math.log2(math.e)
FLOPS_PER_US = 1.1e9
MARK = jax.ShapeDtypeStruct((8, LANES), jnp.float32)
GROUP_OUT = (GROUP * HEAD_DIM + LANES - 1) // LANES * LANES
WHOLE = pl.BlockSpec(memory_space=pltpu.VMEM)
ANYWHERE = pl.BlockSpec(memory_space=pl.ANY)


def ring_order(count):
    return list(range(0, count, 2)) + list(range(count - 1, 0, -2))


def ring_pairs(count):
    order = ring_order(count)
    ahead = [(order[i], order[(i + 1) % count]) for i in range(count)]
    return ahead, [(b, a) for a, b in ahead]


def ring_starts(count, rows):
    order = ring_order(count)
    place = {owner: i for i, owner in enumerate(order)}
    table = []
    for mine in range(count):
        starts = [mine * rows]
        for step in range(1, count // 2):
            starts.append(order[(place[mine] - step) % count] * rows)
            starts.append(order[(place[mine] + step) % count] * rows)
        opposite = order[(place[mine] + count // 2) % count] * rows
        table.append(starts + [opposite])
    return np.array(table, np.int32)


def kernel_call(body, name, room, micros, **kwargs):
    return pl.pallas_call(
        body,
        compiler_params=pltpu.CompilerParams(vmem_limit_bytes=room * 1024 * 1024),
        cost_estimate=pl.CostEstimate(flops=int(micros * FLOPS_PER_US), bytes_accessed=0, transcendentals=0),
        name=name,
        **kwargs,
    )


def tie(value, *earlier):
    return lax.optimization_barrier((value, *earlier))[0]


def normalize_kernel(count, first_chunk, scalars, *refs):
    chunks, gain_ref = refs[:count], refs[count]
    out_ref, mark_ref, stage, sems = refs[-4:]
    mark_ref[...] = jnp.zeros(mark_ref.shape, jnp.float32)
    copies = []
    for j in range(count):
        rows = chunks[j].shape[0]
        values = chunks[j][...].astype(jnp.float32)
        meansq = jnp.mean(values * values, axis=-1, keepdims=True)
        scaled = values * lax.rsqrt(meansq + 1e-05) * gain_ref[...]
        stage[j] = scaled.astype(jnp.bfloat16)
        place = pl.multiple_of(scalars[2 + first_chunk + j], 16)
        copies.append(pltpu.make_async_copy(stage.at[j], out_ref.at[pl.ds(place, rows), :], sems.at[j]))
        copies[-1].start()
    for copy in copies:
        copy.wait()


def normalize_some(scalars, first_chunk, chunks, gain, total, into=None):
    rows, width = chunks[0].shape
    count = len(chunks)
    more = [] if into is None else [into]
    return kernel_call(
        functools.partial(normalize_kernel, count, first_chunk),
        "normalize",
        16,
        0.05,
        grid_spec=pltpu.PrefetchScalarGridSpec(
            num_scalar_prefetch=1,
            grid=(),
            in_specs=[WHOLE] * (count + 1) + [ANYWHERE] * len(more),
            out_specs=[ANYWHERE, WHOLE],
            scratch_shapes=[
                pltpu.VMEM((count, rows, width), jnp.bfloat16),
                pltpu.SemaphoreType.DMA((count,)),
            ],
        ),
        out_shape=[jax.ShapeDtypeStruct((total, width), jnp.bfloat16), MARK],
        input_output_aliases={count + 2: 0} if more else {},
    )(scalars, *chunks, gain.reshape(1, width), *more)


def window_at(wide, start):
    base = start // LANES * LANES
    if start + HEAD_DIM <= base + LANES:
        view = wide[:, base : base + LANES]
        return view if start == base else pltpu.roll(view, LANES - (start - base), 1)
    view = wide[:, base : base + 2 * LANES]
    return pltpu.roll(view, view.shape[1] - (start - base), 1)[:, :LANES]


def widen(values):
    rows, width = values.shape
    padded = (width + LANES - 1) // LANES * LANES
    if padded == width:
        return values
    return jnp.concatenate([values, jnp.zeros((rows, padded - width), values.dtype)], axis=1)


def project_kernel(pieces, first_piece, groups, scalars, *refs):
    normed_ref, cos_ref, sin_ref = refs[:3]
    parts = refs[3 : 3 + pieces]
    query_ref, new_ref, written_ref, mark_ref = refs[3 + pieces : 7 + pieces]
    weight, part_sems = refs[7 + pieces :]
    mark_ref[...] = jnp.zeros(mark_ref.shape, jnp.float32)
    copies = []
    for i in range(pieces):
        rows = parts[i].shape[0]
        place = pl.multiple_of(scalars[first_piece + i], 16)
        copies.append(
            pltpu.make_async_copy(parts[i], weight.at[pl.ds(place, rows), :], part_sems.at[i])
        )
        copies[-1].start()
    for copy in copies:
        copy.wait()
    lane = lax.broadcasted_iota(jnp.int32, (1, LANES), 1)
    middle = (weight.shape[1] // 2 + LANES - 1) // LANES * LANES
    projected = widen(
        jnp.concatenate(
            [
                jnp.dot(normed_ref[...], weight[:, columns], preferred_element_type=jnp.float32)
                for columns in (slice(0, middle), slice(middle, weight.shape[1]))
            ],
            axis=1,
        )
    )
    total = projected.shape[0]
    cosine, sine = cos_ref[...], sin_ref[...]
    live = lax.broadcasted_iota(jnp.int32, (1, total), 1) < scalars[0]
    for g in range(groups):
        for i in range(GROUP + 2):
            head = window_at(projected, (g * (GROUP + 2) + i) * HEAD_DIM)
            if i <= GROUP:
                swapped = jnp.where(
                    lane < HEAD_DIM // 2,
                    pltpu.roll(head, LANES - HEAD_DIM // 2, 1),
                    pltpu.roll(head, HEAD_DIM // 2, 1),
                )
                head = head * cosine + swapped * sine
            if i < GROUP:
                query_ref[g * GROUP + i] = head.astype(jnp.bfloat16)
            else:
                turned = jnp.transpose(head)[:HEAD_DIM, :]
                first = (2 * g + i - GROUP) * HEAD_DIM
                rows = slice(first, first + HEAD_DIM)
                new_ref[rows, :] = turned.astype(jnp.bfloat16)
                written_ref[rows, :] = jnp.where(live, turned, 0.0).astype(jnp.bfloat16)


def project(scalars, first_piece, normed, cosine, sine, pieces):
    total, width = normed.shape
    columns = pieces[0].shape[1]
    groups = columns // ((GROUP + 2) * HEAD_DIM)
    count = len(pieces)
    return kernel_call(
        functools.partial(project_kernel, count, first_piece, groups),
        "project",
        32,
        8,
        grid_spec=pltpu.PrefetchScalarGridSpec(
            num_scalar_prefetch=1,
            grid=(),
            in_specs=[WHOLE] * 3 + [ANYWHERE] * count,
            out_specs=[WHOLE] * 4,
            scratch_shapes=[
                pltpu.VMEM((width, columns), jnp.bfloat16),
                pltpu.SemaphoreType.DMA((count,)),
            ],
        ),
        out_shape=[
            jax.ShapeDtypeStruct((groups * GROUP, total, LANES), jnp.bfloat16),
            jax.ShapeDtypeStruct((groups * 2 * HEAD_DIM, total), jnp.bfloat16),
            jax.ShapeDtypeStruct((groups * 2 * HEAD_DIM, total), jnp.bfloat16),
            MARK,
        ],
    )(scalars, normed, cosine, sine, *pieces)


def attend_kernel(extras, group, begin_chunk, count, chunk, scalars, *refs):
    query_ref, cache_ref, new_ref = refs[:3]
    out_ref = refs[3 + extras]
    keys, values, sems = refs[4 + extras :]
    length, prefix = scalars[0], scalars[1]
    rows = GROUP * chunk
    oldest = WINDOW - prefix
    lane = lax.broadcasted_iota(jnp.int32, (1, VALUE_ROWS), 1)
    factor = SCORE_SCALE * LOG2E
    offset = group * GROUP * HEAD_DIM % LANES
    total_slots = keys.shape[1]
    span = (chunk + LANES - 1) // LANES * LANES
    head_rows = pl.ds(0, HEAD_DIM)
    spans = [(WINDOW, total_slots - WINDOW)] + [(i, KEY_TILE) for i in range(0, WINDOW, KEY_TILE)]
    copies = []
    for n, (start, size) in enumerate(spans):
        for k, room in enumerate((keys, values)):
            if n == 0:
                source = new_ref.at[pl.ds((2 * group + k) * HEAD_DIM, HEAD_DIM), :]
            else:
                source = cache_ref.at[pl.ds((2 * group + k) * HEAD_DIM, HEAD_DIM), pl.ds(start, size)]
            copies.append(
                pltpu.make_async_copy(source, room.at[head_rows, pl.ds(start, size)], sems.at[2 * n + k])
            )
            copies[-1].start()
    ones = lax.broadcasted_iota(jnp.int32, (VALUE_ROWS - HEAD_DIM, total_slots), 0) == 0
    values[HEAD_DIM:, :] = ones.astype(jnp.float32).astype(jnp.bfloat16)
    for copy in copies[:2]:
        copy.wait()
    for copy in copies[2:]:
        copy.wait()

    def one_chunk(j, unused):
        first = pl.multiple_of(scalars[2 + begin_chunk + j], 16)
        base = pl.multiple_of(first // LANES * LANES, LANES)
        here = pl.ds(pl.multiple_of(j * chunk, 16), chunk)

        @pl.when(first >= length)
        def _():
            out_ref[here, :] = jnp.zeros((chunk, GROUP_OUT), jnp.bfloat16)

        @pl.when(first < length)
        def _():
            query = query_ref[:, pl.ds(first, chunk), :].reshape(rows, LANES)[:, :HEAD_DIM]
            token = lax.broadcasted_iota(jnp.int32, (GROUP, chunk, 1), 1).reshape(rows, 1) + first

            def scores_of(start, size):
                return jnp.dot(query, keys[:, pl.ds(start, size)], preferred_element_type=jnp.float32)

            ahead_of = lax.broadcasted_iota(jnp.int32, (1, span), 1) - (token - base)

            def recent(scores):
                return jnp.where(ahead_of <= 0, scores, -jnp.inf)

            def oldest_in(scores, start):
                slot = lax.broadcasted_iota(jnp.int32, (1, KEY_TILE), 1) + start
                scores = jnp.where(slot >= oldest, scores, -jnp.inf)
                edge = jnp.where(ahead_of + (start - base) > 0, scores[:, :span], -jnp.inf)
                return jnp.concatenate([edge, scores[:, span:]], axis=1)

            def fold(scores, start, size, carry):
                top, total = carry
                new_top = jnp.maximum(top, jnp.max(scores, axis=1, keepdims=True))
                weights = jnp.exp2((scores - new_top) * factor).astype(jnp.bfloat16)
                shrink = jnp.exp2((top - new_top) * factor)
                added = lax.dot_general(
                    weights,
                    values[:, pl.ds(start, size)],
                    (((1,), (1,)), ((), ())),
                    preferred_element_type=jnp.float32,
                )
                return new_top, total * shrink + added

            def finish(total):
                result = total / total[:, HEAD_DIM : HEAD_DIM + 1]
                result = jnp.where((token < length) & (lane < HEAD_DIM), result, 0.0)
                rest = jnp.zeros((rows, 2 * LANES - VALUE_ROWS), jnp.float32)
                result = jnp.concatenate([result, rest], axis=1).reshape(GROUP, chunk, 2 * LANES)
                columns = [None] * (GROUP_OUT // LANES + 1)
                for i in range(GROUP):
                    start = offset + i * HEAD_DIM
                    base, shift = start // LANES, start % LANES
                    pair = pltpu.roll(result[i], shift, 1) if shift else result[i]
                    for k in range(2):
                        piece = pair[:, k * LANES : (k + 1) * LANES]
                        old = columns[base + k]
                        columns[base + k] = piece if old is None else old + piece
                wide = jnp.concatenate(columns[: GROUP_OUT // LANES], axis=1)
                out_ref[here, :] = wide.astype(jnp.bfloat16)

            def at(i):
                return pl.multiple_of(base + i * KEY_TILE, LANES)

            newest = at(WINDOW // KEY_TILE)
            none = (
                jnp.full((rows, 1), -1e38, jnp.float32),
                jnp.zeros((rows, VALUE_ROWS), jnp.float32),
            )
            begin = jnp.clip((oldest - base) // KEY_TILE, 0, WINDOW // KEY_TILE - 1)

            @pl.when(begin == 0)
            def _():
                scores = recent(scores_of(newest, span))
                start, size, carry = newest, span, none
                for i in range(WINDOW // KEY_TILE):
                    coming = scores_of(at(i), KEY_TILE)
                    if i == 0:
                        coming = oldest_in(coming, at(0))
                    carry = fold(scores, start, size, carry)
                    scores, start, size = coming, at(i), KEY_TILE
                finish(fold(scores, start, size, carry)[1])

            @pl.when(begin > 0)
            def _():
                carry = fold(recent(scores_of(newest, span)), newest, span, none)
                carry = fold(oldest_in(scores_of(at(begin), KEY_TILE), at(begin)), at(begin), KEY_TILE, carry)

                def step(i, c):
                    return fold(scores_of(at(i), KEY_TILE), at(i), KEY_TILE, c)

                finish(lax.fori_loop(begin + 1, WINDOW // KEY_TILE, step, carry)[1])

        return unused

    lax.fori_loop(0, count, one_chunk, 0)


def attend(scalars, query, cache, new, group, half, chunk, extras=()):
    total = query.shape[1]
    rows = total // 2
    count = rows // chunk
    slots = WINDOW + total
    return kernel_call(
        functools.partial(attend_kernel, len(extras), group, half * count, count, chunk),
        "attend",
        32,
        10,
        grid_spec=pltpu.PrefetchScalarGridSpec(
            num_scalar_prefetch=1,
            grid=(1,),
            in_specs=[pl.BlockSpec((GROUP, total, LANES), lambda i, s: (group, 0, 0))]
            + [ANYWHERE] * (2 + len(extras)),
            out_specs=pl.BlockSpec((rows, GROUP_OUT), lambda i, s: (0, 0)),
            scratch_shapes=[
                pltpu.VMEM((HEAD_DIM, slots), jnp.bfloat16),
                pltpu.VMEM((VALUE_ROWS, slots), jnp.bfloat16),
                pltpu.SemaphoreType.DMA((2 * (1 + WINDOW // KEY_TILE),)),
            ],
        ),
        out_shape=jax.ShapeDtypeStruct((rows, GROUP_OUT), jnp.bfloat16),
    )(scalars, query, cache, new, *extras)


def output_kernel(groups, pieces, first_piece, scalars, *refs):
    attended = refs[:groups]
    parts = refs[groups : groups + pieces]
    out_refs = refs[groups + pieces : -2]
    weight, sems = refs[-2:]
    copies = []
    for i in range(pieces):
        rows = parts[i].shape[0]
        place = pl.multiple_of(scalars[first_piece + i], 16)
        copies.append(pltpu.make_async_copy(parts[i], weight.at[pl.ds(place, rows), :], sems.at[i]))
        copies[-1].start()
    for copy in copies:
        copy.wait()
    depth = weight.shape[1]
    columns = [None] * (depth // LANES + 1)
    for g in range(groups):
        base = g * GROUP * HEAD_DIM // LANES
        for k in range(GROUP_OUT // LANES):
            piece = attended[g][:, k * LANES : (k + 1) * LANES]
            old = columns[base + k]
            columns[base + k] = piece if old is None else old + piece
    used = (depth + LANES - 1) // LANES
    left = jnp.concatenate(columns[:used], axis=1)[:, :depth]
    product = lax.dot_general(
        left, weight[...], (((1,), (1,)), ((), ())), preferred_element_type=jnp.float32
    )
    row = 0
    for out in out_refs:
        out[...] = product[row : row + out.shape[0], :].astype(out.dtype)
        row += out.shape[0]


def output_products(scalars, first_piece, attended, pieces, outs):
    count = len(pieces)
    rows = attended[0].shape[0]
    depth = pieces[0].shape[1]
    width = sum(p.shape[0] for p in pieces)
    return kernel_call(
        functools.partial(output_kernel, len(attended), count, first_piece),
        "output",
        28,
        4.5,
        grid_spec=pltpu.PrefetchScalarGridSpec(
            num_scalar_prefetch=1,
            grid=(),
            in_specs=[WHOLE] * len(attended) + [ANYWHERE] * count,
            out_specs=[WHOLE] * len(outs),
            scratch_shapes=[
                pltpu.VMEM((width, depth), jnp.bfloat16),
                pltpu.SemaphoreType.DMA((count,)),
            ],
        ),
        out_shape=[jax.ShapeDtypeStruct((r, width), kind) for r, kind in outs],
    )(scalars, *attended, *pieces)


def rotation_tables(position):
    halfway = HEAD_DIM // 2
    frequency = jnp.exp(
        jnp.arange(halfway, dtype=jnp.float32) * (-2.0 * math.log(10000.0) / HEAD_DIM)
    )
    angles = position.astype(jnp.float32)[..., None] * frequency
    cosine, sine = jnp.cos(angles), jnp.sin(angles)
    rest = jnp.zeros((position.shape[0], LANES - HEAD_DIM), jnp.float32)
    return (
        jnp.concatenate([cosine, cosine, rest], axis=1),
        jnp.concatenate([-sine, sine, rest], axis=1),
    )


def shards(hidden, norm_gain, w_qkv, w_out, kv_cache, new_len, prefix_len):
    seq_index = lax.axis_index("seq")
    head_index = lax.axis_index("head")
    seq_count = lax.axis_size("seq")
    head_count = lax.axis_size("head")
    unused_lead, chunk, width = hidden.shape
    depth, total_cols = w_qkv.shape
    groups = total_cols // ((GROUP + 2) * HEAD_DIM) // head_count
    group_width = (GROUP + 2) * HEAD_DIM
    head_cols = groups * GROUP * HEAD_DIM
    out_depth = w_out.shape[1]
    new_total = head_count * chunk
    paired = head_count == 4
    core_pairs = [(i, i ^ 1) for i in range(head_count)]
    y_pairs = [(i, i ^ 2) for i in range(head_count)]

    if paired:
        order = np.array([[h ^ j for j in range(head_count)] for h in range(head_count)])
    else:
        order = np.array([[(h + j) % head_count for j in range(head_count)] for h in range(head_count)])
    ring_table = np.concatenate([ring_starts(seq_count, depth), ring_starts(seq_count, out_depth)], axis=1)
    place_table = np.concatenate(
        [
            np.zeros((seq_count * head_count, 2), np.int32),
            np.tile((order * chunk).astype(np.int32), (seq_count, 1)),
            np.repeat(ring_table, head_count, axis=0),
        ],
        axis=1,
    )
    places = lax.dynamic_index_in_dim(
        jnp.asarray(place_table), seq_index * head_count + head_index, 0, keepdims=False
    )
    length = lax.dynamic_index_in_dim(new_len, seq_index, 0)
    prefix = lax.dynamic_index_in_dim(prefix_len, seq_index, 0)
    scalars = jnp.concatenate([length, prefix, places[2:]])
    first_qkv = 2 + head_count
    first_out = first_qkv + seq_count

    own_hidden = hidden.reshape(chunk, width)
    if paired:
        far = lax.ppermute(own_hidden, "head", y_pairs)
        last = lax.ppermute(far, "head", core_pairs)
    else:
        gathered = lax.all_gather(own_hidden, "head", axis=0)
        chunks = [
            lax.dynamic_index_in_dim(gathered, (head_index + j) % head_count, 0, keepdims=False)
            for j in range(head_count)
        ]
        far = last = gathered

    ahead, back = ring_pairs(seq_count)
    own_cols = lax.dynamic_slice_in_dim(
        w_qkv, head_index * groups * group_width, groups * group_width, 1
    )
    pieces = [own_cols]
    f = b = own_cols
    cosine, sine = rotation_tables(prefix[0] + jnp.arange(new_total, dtype=jnp.int32))
    final = seq_count // 2
    count = head_count // 2
    for step in range(1, final + 1):
        if step == 2:
            if paired:
                chunks = [own_hidden, lax.ppermute(tie(own_hidden, f), "head", core_pairs), far, last]
            normed, mark = normalize_some(places, 0, chunks[:count], norm_gain, new_total)
        elif step == final - 1:
            f, b = lax.optimization_barrier((f, b, far, mark))[:2]
        elif step == final:
            normed, mark = normalize_some(
                places, count, chunks[count:], norm_gain, new_total, normed
            )
            third = (f, b)
        f = lax.ppermute(f, "seq", ahead)
        if step < final:
            b = lax.ppermute(b, "seq", back)
        pieces += [f, b] if step < final else [f]

    cache = kv_cache.reshape(WINDOW, kv_cache.shape[-1]).T

    out_rows = lax.dynamic_slice_in_dim(w_out, head_index * head_cols, head_cols, 0).T
    out_rows = tie(out_rows, *third)
    attended = [[None] * groups, [None] * groups]
    out_pieces = [out_rows]
    ready = pieces[-1]
    f = b = out_rows
    for step in range(1, final + 1):
        moved = []
        if step > 1:
            f, b = lax.optimization_barrier((f, b, ready))[:2]
            f = lax.ppermute(f, "seq", ahead)
            moved.append(f)
        b = lax.ppermute(b, "seq", back)
        moved.append(b)
        out_pieces += moved
        here = tie(scalars, *moved)
        if step == 1:
            query, new, written, projected = project(here, first_qkv, normed, cosine, sine, pieces)
        elif step == 2:
            ready = projected
        if 1 < step < 2 + groups:
            attended[1][step - 2] = attend(here, query, cache, new, step - 2, 1, chunk)
        if 2 < step < 3 + groups:
            ready = attended[1][step - 3]
    out_pieces = (
        out_pieces[:1]
        + [p for k in range(1, final) for p in (out_pieces[2 * k], out_pieces[2 * k - 1])]
        + out_pieces[-1:]
    )
    for g in range(groups):
        if attended[1][g] is None:
            attended[1][g] = attend(scalars, query, cache, new, g, 1, chunk)
    late = scalars
    arrived = []
    for g in range(groups):
        if paired and g == 0:
            forth, across = output_products(
                scalars, first_out, attended[1], out_pieces, [(chunk, jnp.bfloat16)] * 2
            )
            beside = lax.ppermute(across, "head", core_pairs)
            both = (forth.astype(jnp.float32) + beside.astype(jnp.float32)).astype(jnp.bfloat16)
            cut = (width * 9 // 20 + LANES - 1) // LANES * LANES
            parts = [both[:, :cut], both[:, cut : 2 * cut], both[:, 2 * cut :]]
            late = tie(scalars, *parts)
        attended[0][g] = attend(late, query, cache, new, g, 0, chunk)
        if paired:
            part = tie(parts[g], *attended[0][:g])
            arrived.append(lax.ppermute(part, "head", y_pairs))
            late = tie(late, arrived[g], attended[0][g])
    kv_written = written.T.reshape(1, new_total, groups * 2 * HEAD_DIM)

    if paired:
        own, other = output_products(
            late, first_out, attended[0], out_pieces, [(chunk, jnp.float32), (chunk, jnp.bfloat16)]
        )
        arrived += [lax.ppermute(part, "head", y_pairs) for part in parts[groups:]]
        near = lax.ppermute(other, "head", core_pairs)
        far = jnp.concatenate(arrived, axis=1)
        output = own + near.astype(jnp.float32) + far.astype(jnp.float32)
    else:
        products = [
            output_products(scalars, first_out, part, out_pieces, [(new_total // 2, jnp.bfloat16)])[0]
            for part in attended
        ]
        stacked = jnp.concatenate(products, axis=0).reshape(head_count, chunk, width)
        back = jnp.asarray((np.arange(head_count)[None] - np.arange(head_count)[:, None]) % head_count)
        output = lax.psum_scatter(stacked[back[head_index]], "head", scatter_dimension=0)
    return (output.astype(jnp.bfloat16).reshape(1, chunk, width), kv_written)


def solution(mesh):
    placed = (
        P("seq", "head", None),
        P(),
        P("seq", None),
        P(None, "seq"),
        P("seq", None, "head"),
        P(),
        P(),
    )
    return jax.shard_map(
        shards,
        mesh=mesh,
        in_specs=placed,
        out_specs=(P("seq", "head", None), P("seq", None, "head")),
        check_vma=False,
    )
```

```python
import functools
import math

import jax
import jax.numpy as jnp
import numpy as np
from jax import lax
from jax.experimental import pallas as pl
from jax.experimental.pallas import tpu as pltpu
from jax.sharding import PartitionSpec as P

HEAD_DIM = 80
WINDOW = 4096
GROUP = 4
LANES = 128
KEY_TILE = 1024
VALUE_ROWS = HEAD_DIM + 16
SCORE_SCALE = 1.0 / math.sqrt(HEAD_DIM)
LOG2E = math.log2(math.e)
FLOPS_PER_US = 1.1e9
MARK = jax.ShapeDtypeStruct((8, LANES), jnp.float32)
GROUP_OUT = (GROUP * HEAD_DIM + LANES - 1) // LANES * LANES
WHOLE = pl.BlockSpec(memory_space=pltpu.VMEM)
ANYWHERE = pl.BlockSpec(memory_space=pl.ANY)


def ring_order(count):
    return list(range(0, count, 2)) + list(range(count - 1, 0, -2))


def ring_pairs(count):
    order = ring_order(count)
    ahead = [(order[i], order[(i + 1) % count]) for i in range(count)]
    return ahead, [(b, a) for a, b in ahead]


def ring_starts(count, rows):
    order = ring_order(count)
    place = {owner: i for i, owner in enumerate(order)}
    table = []
    for mine in range(count):
        starts = [mine * rows]
        for step in range(1, count // 2):
            starts.append(order[(place[mine] - step) % count] * rows)
            starts.append(order[(place[mine] + step) % count] * rows)
        opposite = order[(place[mine] + count // 2) % count] * rows
        table.append(starts + [opposite])
    return np.array(table, np.int32)


def kernel_call(body, name, room, micros, **kwargs):
    return pl.pallas_call(
        body,
        compiler_params=pltpu.CompilerParams(vmem_limit_bytes=room * 1024 * 1024),
        cost_estimate=pl.CostEstimate(flops=int(micros * FLOPS_PER_US), bytes_accessed=0, transcendentals=0),
        name=name,
        **kwargs,
    )


def tie(value, *earlier):
    return lax.optimization_barrier((value, *earlier))[0]


def normalize_kernel(count, first_chunk, scalars, *refs):
    chunks, gain_ref = refs[:count], refs[count]
    out_ref, mark_ref, stage, sems = refs[-4:]
    mark_ref[...] = jnp.zeros(mark_ref.shape, jnp.float32)
    copies = []
    for j in range(count):
        rows = chunks[j].shape[0]
        values = chunks[j][...].astype(jnp.float32)
        meansq = jnp.mean(values * values, axis=-1, keepdims=True)
        scaled = values * lax.rsqrt(meansq + 1e-05) * gain_ref[...]
        stage[j] = scaled.astype(jnp.bfloat16)
        place = pl.multiple_of(scalars[2 + first_chunk + j], 16)
        copies.append(pltpu.make_async_copy(stage.at[j], out_ref.at[pl.ds(place, rows), :], sems.at[j]))
        copies[-1].start()
    for copy in copies:
        copy.wait()


def normalize_some(scalars, first_chunk, chunks, gain, total, into=None):
    rows, width = chunks[0].shape
    count = len(chunks)
    more = [] if into is None else [into]
    return kernel_call(
        functools.partial(normalize_kernel, count, first_chunk),
        "normalize",
        16,
        0.05,
        grid_spec=pltpu.PrefetchScalarGridSpec(
            num_scalar_prefetch=1,
            grid=(),
            in_specs=[WHOLE] * (count + 1) + [ANYWHERE] * len(more),
            out_specs=[ANYWHERE, WHOLE],
            scratch_shapes=[
                pltpu.VMEM((count, rows, width), jnp.bfloat16),
                pltpu.SemaphoreType.DMA((count,)),
            ],
        ),
        out_shape=[jax.ShapeDtypeStruct((total, width), jnp.bfloat16), MARK],
        input_output_aliases={count + 2: 0} if more else {},
    )(scalars, *chunks, gain.reshape(1, width), *more)


def window_at(wide, start):
    base = start // LANES * LANES
    if start + HEAD_DIM <= base + LANES:
        view = wide[:, base : base + LANES]
        return view if start == base else pltpu.roll(view, LANES - (start - base), 1)
    view = wide[:, base : base + 2 * LANES]
    return pltpu.roll(view, view.shape[1] - (start - base), 1)[:, :LANES]


def widen(values):
    rows, width = values.shape
    padded = (width + LANES - 1) // LANES * LANES
    if padded == width:
        return values
    return jnp.concatenate([values, jnp.zeros((rows, padded - width), values.dtype)], axis=1)


def project_kernel(pieces, first_piece, groups, scalars, *refs):
    normed_ref, cos_ref, sin_ref = refs[:3]
    parts = refs[3 : 3 + pieces]
    query_ref, new_ref, written_ref, mark_ref = refs[3 + pieces : 7 + pieces]
    weight, part_sems = refs[7 + pieces :]
    mark_ref[...] = jnp.zeros(mark_ref.shape, jnp.float32)
    copies = []
    for i in range(pieces):
        rows = parts[i].shape[0]
        place = pl.multiple_of(scalars[first_piece + i], 16)
        copies.append(
            pltpu.make_async_copy(parts[i], weight.at[pl.ds(place, rows), :], part_sems.at[i])
        )
        copies[-1].start()
    for copy in copies:
        copy.wait()
    lane = lax.broadcasted_iota(jnp.int32, (1, LANES), 1)
    middle = (weight.shape[1] // 2 + LANES - 1) // LANES * LANES
    projected = widen(
        jnp.concatenate(
            [
                jnp.dot(normed_ref[...], weight[:, columns], preferred_element_type=jnp.float32)
                for columns in (slice(0, middle), slice(middle, weight.shape[1]))
            ],
            axis=1,
        )
    )
    total = projected.shape[0]
    cosine, sine = cos_ref[...], sin_ref[...]
    live = lax.broadcasted_iota(jnp.int32, (1, total), 1) < scalars[0]
    for g in range(groups):
        for i in range(GROUP + 2):
            head = window_at(projected, (g * (GROUP + 2) + i) * HEAD_DIM)
            if i <= GROUP:
                swapped = jnp.where(
                    lane < HEAD_DIM // 2,
                    pltpu.roll(head, LANES - HEAD_DIM // 2, 1),
                    pltpu.roll(head, HEAD_DIM // 2, 1),
                )
                head = head * cosine + swapped * sine
            if i < GROUP:
                query_ref[g * GROUP + i] = head.astype(jnp.bfloat16)
            else:
                turned = jnp.transpose(head)[:HEAD_DIM, :]
                first = (2 * g + i - GROUP) * HEAD_DIM
                rows = slice(first, first + HEAD_DIM)
                new_ref[rows, :] = turned.astype(jnp.bfloat16)
                written_ref[rows, :] = jnp.where(live, turned, 0.0).astype(jnp.bfloat16)


def project(scalars, first_piece, normed, cosine, sine, pieces):
    total, width = normed.shape
    columns = pieces[0].shape[1]
    groups = columns // ((GROUP + 2) * HEAD_DIM)
    count = len(pieces)
    return kernel_call(
        functools.partial(project_kernel, count, first_piece, groups),
        "project",
        32,
        8,
        grid_spec=pltpu.PrefetchScalarGridSpec(
            num_scalar_prefetch=1,
            grid=(),
            in_specs=[WHOLE] * 3 + [ANYWHERE] * count,
            out_specs=[WHOLE] * 4,
            scratch_shapes=[
                pltpu.VMEM((width, columns), jnp.bfloat16),
                pltpu.SemaphoreType.DMA((count,)),
            ],
        ),
        out_shape=[
            jax.ShapeDtypeStruct((groups * GROUP, total, LANES), jnp.bfloat16),
            jax.ShapeDtypeStruct((groups * 2 * HEAD_DIM, total), jnp.bfloat16),
            jax.ShapeDtypeStruct((groups * 2 * HEAD_DIM, total), jnp.bfloat16),
            MARK,
        ],
    )(scalars, normed, cosine, sine, *pieces)


def attend_kernel(extras, group, begin_chunk, count, chunk, scalars, *refs):
    query_ref, cache_ref, new_ref = refs[:3]
    out_ref = refs[3 + extras]
    keys, values, sems = refs[4 + extras :]
    length, prefix = scalars[0], scalars[1]
    rows = GROUP * chunk
    oldest = WINDOW - prefix
    lane = lax.broadcasted_iota(jnp.int32, (1, VALUE_ROWS), 1)
    factor = SCORE_SCALE * LOG2E
    offset = group * GROUP * HEAD_DIM % LANES
    total_slots = keys.shape[1]
    span = (chunk + LANES - 1) // LANES * LANES
    head_rows = pl.ds(0, HEAD_DIM)
    spans = [(WINDOW, total_slots - WINDOW)] + [(i, KEY_TILE) for i in range(0, WINDOW, KEY_TILE)]
    copies = []
    for n, (start, size) in enumerate(spans):
        for k, room in enumerate((keys, values)):
            if n == 0:
                source = new_ref.at[pl.ds((2 * group + k) * HEAD_DIM, HEAD_DIM), :]
            else:
                source = cache_ref.at[pl.ds((2 * group + k) * HEAD_DIM, HEAD_DIM), pl.ds(start, size)]
            copies.append(
                pltpu.make_async_copy(source, room.at[head_rows, pl.ds(start, size)], sems.at[2 * n + k])
            )
            copies[-1].start()
    ones = lax.broadcasted_iota(jnp.int32, (VALUE_ROWS - HEAD_DIM, total_slots), 0) == 0
    values[HEAD_DIM:, :] = ones.astype(jnp.float32).astype(jnp.bfloat16)
    for copy in copies[:2]:
        copy.wait()
    for copy in copies[2:]:
        copy.wait()

    def one_chunk(j, unused):
        first = pl.multiple_of(scalars[2 + begin_chunk + j], 16)
        base = pl.multiple_of(first // LANES * LANES, LANES)
        here = pl.ds(pl.multiple_of(j * chunk, 16), chunk)

        @pl.when(first >= length)
        def _():
            out_ref[here, :] = jnp.zeros((chunk, GROUP_OUT), jnp.bfloat16)

        @pl.when(first < length)
        def _():
            query = query_ref[:, pl.ds(first, chunk), :].reshape(rows, LANES)[:, :HEAD_DIM]
            token = lax.broadcasted_iota(jnp.int32, (GROUP, chunk, 1), 1).reshape(rows, 1) + first

            def scores_of(start, size):
                return jnp.dot(query, keys[:, pl.ds(start, size)], preferred_element_type=jnp.float32)

            ahead_of = lax.broadcasted_iota(jnp.int32, (1, span), 1) - (token - base)

            def recent(scores):
                return jnp.where(ahead_of <= 0, scores, -jnp.inf)

            def oldest_in(scores, start):
                slot = lax.broadcasted_iota(jnp.int32, (1, KEY_TILE), 1) + start
                scores = jnp.where(slot >= oldest, scores, -jnp.inf)
                edge = jnp.where(ahead_of + (start - base) > 0, scores[:, :span], -jnp.inf)
                return jnp.concatenate([edge, scores[:, span:]], axis=1)

            def fold(scores, start, size, carry):
                top, total = carry
                new_top = jnp.maximum(top, jnp.max(scores, axis=1, keepdims=True))
                weights = jnp.exp2((scores - new_top) * factor).astype(jnp.bfloat16)
                shrink = jnp.exp2((top - new_top) * factor)
                added = lax.dot_general(
                    weights,
                    values[:, pl.ds(start, size)],
                    (((1,), (1,)), ((), ())),
                    preferred_element_type=jnp.float32,
                )
                return new_top, total * shrink + added

            def finish(total):
                result = total / total[:, HEAD_DIM : HEAD_DIM + 1]
                result = jnp.where((token < length) & (lane < HEAD_DIM), result, 0.0)
                rest = jnp.zeros((rows, 2 * LANES - VALUE_ROWS), jnp.float32)
                result = jnp.concatenate([result, rest], axis=1).reshape(GROUP, chunk, 2 * LANES)
                columns = [None] * (GROUP_OUT // LANES + 1)
                for i in range(GROUP):
                    start = offset + i * HEAD_DIM
                    base, shift = start // LANES, start % LANES
                    pair = pltpu.roll(result[i], shift, 1) if shift else result[i]
                    for k in range(2):
                        piece = pair[:, k * LANES : (k + 1) * LANES]
                        old = columns[base + k]
                        columns[base + k] = piece if old is None else old + piece
                wide = jnp.concatenate(columns[: GROUP_OUT // LANES], axis=1)
                out_ref[here, :] = wide.astype(jnp.bfloat16)

            def at(i):
                return pl.multiple_of(base + i * KEY_TILE, LANES)

            newest = at(WINDOW // KEY_TILE)
            none = (
                jnp.full((rows, 1), -1e38, jnp.float32),
                jnp.zeros((rows, VALUE_ROWS), jnp.float32),
            )
            begin = jnp.clip((oldest - base) // KEY_TILE, 0, WINDOW // KEY_TILE - 1)

            @pl.when(begin == 0)
            def _():
                scores = recent(scores_of(newest, span))
                start, size, carry = newest, span, none
                for i in range(WINDOW // KEY_TILE):
                    coming = scores_of(at(i), KEY_TILE)
                    if i == 0:
                        coming = oldest_in(coming, at(0))
                    carry = fold(scores, start, size, carry)
                    scores, start, size = coming, at(i), KEY_TILE
                finish(fold(scores, start, size, carry)[1])

            @pl.when(begin > 0)
            def _():
                carry = fold(recent(scores_of(newest, span)), newest, span, none)
                carry = fold(oldest_in(scores_of(at(begin), KEY_TILE), at(begin)), at(begin), KEY_TILE, carry)

                def step(i, c):
                    return fold(scores_of(at(i), KEY_TILE), at(i), KEY_TILE, c)

                finish(lax.fori_loop(begin + 1, WINDOW // KEY_TILE, step, carry)[1])

        return unused

    lax.fori_loop(0, count, one_chunk, 0)


def attend(scalars, query, cache, new, group, half, chunk, extras=()):
    total = query.shape[1]
    rows = total // 2
    count = rows // chunk
    slots = WINDOW + total
    return kernel_call(
        functools.partial(attend_kernel, len(extras), group, half * count, count, chunk),
        "attend",
        32,
        10,
        grid_spec=pltpu.PrefetchScalarGridSpec(
            num_scalar_prefetch=1,
            grid=(1,),
            in_specs=[pl.BlockSpec((GROUP, total, LANES), lambda i, s: (group, 0, 0))]
            + [ANYWHERE] * (2 + len(extras)),
            out_specs=pl.BlockSpec((rows, GROUP_OUT), lambda i, s: (0, 0)),
            scratch_shapes=[
                pltpu.VMEM((HEAD_DIM, slots), jnp.bfloat16),
                pltpu.VMEM((VALUE_ROWS, slots), jnp.bfloat16),
                pltpu.SemaphoreType.DMA((2 * (1 + WINDOW // KEY_TILE),)),
            ],
        ),
        out_shape=jax.ShapeDtypeStruct((rows, GROUP_OUT), jnp.bfloat16),
    )(scalars, query, cache, new, *extras)


def output_kernel(groups, pieces, first_piece, scalars, *refs):
    attended = refs[:groups]
    parts = refs[groups : groups + pieces]
    out_refs = refs[groups + pieces : -2]
    weight, sems = refs[-2:]
    copies = []
    for i in range(pieces):
        rows = parts[i].shape[0]
        place = pl.multiple_of(scalars[first_piece + i], 16)
        copies.append(pltpu.make_async_copy(parts[i], weight.at[pl.ds(place, rows), :], sems.at[i]))
        copies[-1].start()
    for copy in copies:
        copy.wait()
    depth = weight.shape[1]
    columns = [None] * (depth // LANES + 1)
    for g in range(groups):
        base = g * GROUP * HEAD_DIM // LANES
        for k in range(GROUP_OUT // LANES):
            piece = attended[g][:, k * LANES : (k + 1) * LANES]
            old = columns[base + k]
            columns[base + k] = piece if old is None else old + piece
    used = (depth + LANES - 1) // LANES
    left = jnp.concatenate(columns[:used], axis=1)[:, :depth]
    product = lax.dot_general(
        left, weight[...], (((1,), (1,)), ((), ())), preferred_element_type=jnp.float32
    )
    row = 0
    for out in out_refs:
        out[...] = product[row : row + out.shape[0], :].astype(out.dtype)
        row += out.shape[0]


def output_products(scalars, first_piece, attended, pieces, outs):
    count = len(pieces)
    rows = attended[0].shape[0]
    depth = pieces[0].shape[1]
    width = sum(p.shape[0] for p in pieces)
    return kernel_call(
        functools.partial(output_kernel, len(attended), count, first_piece),
        "output",
        28,
        4.5,
        grid_spec=pltpu.PrefetchScalarGridSpec(
            num_scalar_prefetch=1,
            grid=(),
            in_specs=[WHOLE] * len(attended) + [ANYWHERE] * count,
            out_specs=[WHOLE] * len(outs),
            scratch_shapes=[
                pltpu.VMEM((width, depth), jnp.bfloat16),
                pltpu.SemaphoreType.DMA((count,)),
            ],
        ),
        out_shape=[jax.ShapeDtypeStruct((r, width), kind) for r, kind in outs],
    )(scalars, *attended, *pieces)


def rotation_tables(position):
    halfway = HEAD_DIM // 2
    frequency = jnp.exp(
        jnp.arange(halfway, dtype=jnp.float32) * (-2.0 * math.log(10000.0) / HEAD_DIM)
    )
    angles = position.astype(jnp.float32)[..., None] * frequency
    cosine, sine = jnp.cos(angles), jnp.sin(angles)
    rest = jnp.zeros((position.shape[0], LANES - HEAD_DIM), jnp.float32)
    return (
        jnp.concatenate([cosine, cosine, rest], axis=1),
        jnp.concatenate([-sine, sine, rest], axis=1),
    )


def shards(hidden, norm_gain, w_qkv, w_out, kv_cache, new_len, prefix_len):
    seq_index = lax.axis_index("seq")
    head_index = lax.axis_index("head")
    seq_count = lax.axis_size("seq")
    head_count = lax.axis_size("head")
    unused_lead, chunk, width = hidden.shape
    depth, total_cols = w_qkv.shape
    groups = total_cols // ((GROUP + 2) * HEAD_DIM) // head_count
    group_width = (GROUP + 2) * HEAD_DIM
    head_cols = groups * GROUP * HEAD_DIM
    out_depth = w_out.shape[1]
    new_total = head_count * chunk
    paired = head_count == 4
    core_pairs = [(i, i ^ 1) for i in range(head_count)]
    y_pairs = [(i, i ^ 2) for i in range(head_count)]

    if paired:
        order = np.array([[h ^ j for j in range(head_count)] for h in range(head_count)])
    else:
        order = np.array([[(h + j) % head_count for j in range(head_count)] for h in range(head_count)])
    ring_table = np.concatenate([ring_starts(seq_count, depth), ring_starts(seq_count, out_depth)], axis=1)
    place_table = np.concatenate(
        [
            np.zeros((seq_count * head_count, 2), np.int32),
            np.tile((order * chunk).astype(np.int32), (seq_count, 1)),
            np.repeat(ring_table, head_count, axis=0),
        ],
        axis=1,
    )
    places = lax.dynamic_index_in_dim(
        jnp.asarray(place_table), seq_index * head_count + head_index, 0, keepdims=False
    )
    length = lax.dynamic_index_in_dim(new_len, seq_index, 0)
    prefix = lax.dynamic_index_in_dim(prefix_len, seq_index, 0)
    scalars = jnp.concatenate([length, prefix, places[2:]])
    first_qkv = 2 + head_count
    first_out = first_qkv + seq_count

    own_hidden = hidden.reshape(chunk, width)
    if paired:
        far = lax.ppermute(own_hidden, "head", y_pairs)
        last = lax.ppermute(far, "head", core_pairs)
    else:
        gathered = lax.all_gather(own_hidden, "head", axis=0)
        chunks = [
            lax.dynamic_index_in_dim(gathered, (head_index + j) % head_count, 0, keepdims=False)
            for j in range(head_count)
        ]
        far = last = gathered

    ahead, back = ring_pairs(seq_count)
    own_cols = lax.dynamic_slice_in_dim(
        w_qkv, head_index * groups * group_width, groups * group_width, 1
    )
    pieces = [own_cols]
    f = b = own_cols
    cosine, sine = rotation_tables(prefix[0] + jnp.arange(new_total, dtype=jnp.int32))
    final = seq_count // 2
    count = head_count // 2
    for step in range(1, final + 1):
        if step == 2:
            if paired:
                chunks = [own_hidden, lax.ppermute(tie(own_hidden, f), "head", core_pairs), far, last]
            normed, mark = normalize_some(places, 0, chunks[:count], norm_gain, new_total)
        elif step == final - 1:
            f, b = lax.optimization_barrier((f, b, far, mark))[:2]
        elif step == final:
            normed, mark = normalize_some(
                places, count, chunks[count:], norm_gain, new_total, normed
            )
            third = (f, b)
        f = lax.ppermute(f, "seq", ahead)
        if step < final:
            b = lax.ppermute(b, "seq", back)
        pieces += [f, b] if step < final else [f]

    cache = kv_cache.reshape(WINDOW, kv_cache.shape[-1]).T

    out_rows = lax.dynamic_slice_in_dim(w_out, head_index * head_cols, head_cols, 0).T
    out_rows = tie(out_rows, *third)
    attended = [[None] * groups, [None] * groups]
    out_pieces = [out_rows]
    ready = pieces[-1]
    f = b = out_rows
    for step in range(1, final + 1):
        moved = []
        if step > 1:
            f, b = lax.optimization_barrier((f, b, ready))[:2]
            f = lax.ppermute(f, "seq", ahead)
            moved.append(f)
        b = lax.ppermute(b, "seq", back)
        moved.append(b)
        out_pieces += moved
        here = tie(scalars, *moved)
        if step == 1:
            query, new, written, projected = project(here, first_qkv, normed, cosine, sine, pieces)
        elif step == 2:
            ready = projected
        if 1 < step < 2 + groups:
            attended[1][step - 2] = attend(here, query, cache, new, step - 2, 1, chunk)
        if 2 < step < 3 + groups:
            ready = attended[1][step - 3]
    out_pieces = (
        out_pieces[:1]
        + [p for k in range(1, final) for p in (out_pieces[2 * k], out_pieces[2 * k - 1])]
        + out_pieces[-1:]
    )
    for g in range(groups):
        if attended[1][g] is None:
            attended[1][g] = attend(scalars, query, cache, new, g, 1, chunk)
    late = scalars
    arrived = []
    for g in range(groups):
        if paired and g == 0:
            forth, across = output_products(
                scalars, first_out, attended[1], out_pieces, [(chunk, jnp.bfloat16)] * 2
            )
            beside = lax.ppermute(across, "head", core_pairs)
            both = (forth.astype(jnp.float32) + beside.astype(jnp.float32)).astype(jnp.bfloat16)
            cut = (width // groups + LANES - 1) // LANES * LANES
            parts = [both[:, k * cut : (k + 1) * cut] for k in range(groups)]
            late = tie(scalars, *parts)
        attended[0][g] = attend(late, query, cache, new, g, 0, chunk)
        if paired:
            part = tie(parts[g], *attended[0][:g])
            arrived.append(lax.ppermute(part, "head", y_pairs))
            late = tie(late, arrived[g], attended[0][g])
    kv_written = written.T.reshape(1, new_total, groups * 2 * HEAD_DIM)

    if paired:
        own, other = output_products(
            late, first_out, attended[0], out_pieces, [(chunk, jnp.float32), (chunk, jnp.bfloat16)]
        )
        near = lax.ppermute(other, "head", core_pairs)
        far = jnp.concatenate(arrived, axis=1)
        output = own + near.astype(jnp.float32) + far.astype(jnp.float32)
    else:
        products = [
            output_products(scalars, first_out, part, out_pieces, [(new_total // 2, jnp.bfloat16)])[0]
            for part in attended
        ]
        stacked = jnp.concatenate(products, axis=0).reshape(head_count, chunk, width)
        back = jnp.asarray((np.arange(head_count)[None] - np.arange(head_count)[:, None]) % head_count)
        output = lax.psum_scatter(stacked[back[head_index]], "head", scatter_dimension=0)
    return (output.astype(jnp.bfloat16).reshape(1, chunk, width), kv_written)


def solution(mesh):
    placed = (
        P("seq", "head", None),
        P(),
        P("seq", None),
        P(None, "seq"),
        P("seq", None, "head"),
        P(),
        P(),
    )
    return jax.shard_map(
        shards,
        mesh=mesh,
        in_specs=placed,
        out_specs=(P("seq", "head", None), P("seq", None, "head")),
        check_vma=False,
    )
```

```python
import functools
import math

import jax
import jax.numpy as jnp
import numpy as np
from jax import lax
from jax.experimental import pallas as pl
from jax.experimental.pallas import tpu as pltpu
from jax.sharding import PartitionSpec as P

HEAD_DIM = 80
WINDOW = 4096
GROUP = 4
LANES = 128
KEY_TILE = 1024
VALUE_ROWS = HEAD_DIM + 16
SCORE_SCALE = 1.0 / math.sqrt(HEAD_DIM)
LOG2E = math.log2(math.e)
FLOPS_PER_US = 1.1e9
MARK = jax.ShapeDtypeStruct((8, LANES), jnp.float32)
GROUP_OUT = (GROUP * HEAD_DIM + LANES - 1) // LANES * LANES
WHOLE = pl.BlockSpec(memory_space=pltpu.VMEM)
ANYWHERE = pl.BlockSpec(memory_space=pl.ANY)


def ring_order(count):
    return list(range(0, count, 2)) + list(range(count - 1, 0, -2))


def ring_pairs(count):
    order = ring_order(count)
    ahead = [(order[i], order[(i + 1) % count]) for i in range(count)]
    return ahead, [(b, a) for a, b in ahead]


def ring_starts(count, rows):
    order = ring_order(count)
    place = {owner: i for i, owner in enumerate(order)}
    table = []
    for mine in range(count):
        starts = [mine * rows]
        for step in range(1, count // 2):
            starts.append(order[(place[mine] - step) % count] * rows)
            starts.append(order[(place[mine] + step) % count] * rows)
        opposite = order[(place[mine] + count // 2) % count] * rows
        table.append(starts + [opposite])
    return np.array(table, np.int32)


def kernel_call(body, name, room, micros, **kwargs):
    return pl.pallas_call(
        body,
        compiler_params=pltpu.CompilerParams(vmem_limit_bytes=room * 1024 * 1024),
        cost_estimate=pl.CostEstimate(flops=int(micros * FLOPS_PER_US), bytes_accessed=0, transcendentals=0),
        name=name,
        **kwargs,
    )


def tie(value, *earlier):
    return lax.optimization_barrier((value, *earlier))[0]


def normalize_kernel(count, first_chunk, scalars, *refs):
    chunks, gain_ref = refs[:count], refs[count]
    out_ref, mark_ref, stage, sems = refs[-4:]
    mark_ref[...] = jnp.zeros(mark_ref.shape, jnp.float32)
    copies = []
    for j in range(count):
        rows = chunks[j].shape[0]
        values = chunks[j][...].astype(jnp.float32)
        meansq = jnp.mean(values * values, axis=-1, keepdims=True)
        scaled = values * lax.rsqrt(meansq + 1e-05) * gain_ref[...]
        stage[j] = scaled.astype(jnp.bfloat16)
        place = pl.multiple_of(scalars[2 + first_chunk + j], 16)
        copies.append(pltpu.make_async_copy(stage.at[j], out_ref.at[pl.ds(place, rows), :], sems.at[j]))
        copies[-1].start()
    for copy in copies:
        copy.wait()


def normalize_some(scalars, first_chunk, chunks, gain, total, into=None):
    rows, width = chunks[0].shape
    count = len(chunks)
    more = [] if into is None else [into]
    return kernel_call(
        functools.partial(normalize_kernel, count, first_chunk),
        "normalize",
        16,
        0.05,
        grid_spec=pltpu.PrefetchScalarGridSpec(
            num_scalar_prefetch=1,
            grid=(),
            in_specs=[WHOLE] * (count + 1) + [ANYWHERE] * len(more),
            out_specs=[ANYWHERE, WHOLE],
            scratch_shapes=[
                pltpu.VMEM((count, rows, width), jnp.bfloat16),
                pltpu.SemaphoreType.DMA((count,)),
            ],
        ),
        out_shape=[jax.ShapeDtypeStruct((total, width), jnp.bfloat16), MARK],
        input_output_aliases={count + 2: 0} if more else {},
    )(scalars, *chunks, gain.reshape(1, width), *more)


def window_at(wide, start):
    base = start // LANES * LANES
    if start + HEAD_DIM <= base + LANES:
        view = wide[:, base : base + LANES]
        return view if start == base else pltpu.roll(view, LANES - (start - base), 1)
    view = wide[:, base : base + 2 * LANES]
    return pltpu.roll(view, view.shape[1] - (start - base), 1)[:, :LANES]


def widen(values):
    rows, width = values.shape
    padded = (width + LANES - 1) // LANES * LANES
    if padded == width:
        return values
    return jnp.concatenate([values, jnp.zeros((rows, padded - width), values.dtype)], axis=1)


def project_kernel(pieces, first_piece, groups, scalars, *refs):
    normed_ref, cos_ref, sin_ref = refs[:3]
    parts = refs[3 : 3 + pieces]
    query_ref, new_ref, written_ref, mark_ref = refs[3 + pieces : 7 + pieces]
    weight, part_sems = refs[7 + pieces :]
    mark_ref[...] = jnp.zeros(mark_ref.shape, jnp.float32)
    copies = []
    for i in range(pieces):
        rows = parts[i].shape[0]
        place = pl.multiple_of(scalars[first_piece + i], 16)
        copies.append(
            pltpu.make_async_copy(parts[i], weight.at[pl.ds(place, rows), :], part_sems.at[i])
        )
        copies[-1].start()
    for copy in copies:
        copy.wait()
    lane = lax.broadcasted_iota(jnp.int32, (1, LANES), 1)
    middle = (weight.shape[1] // 2 + LANES - 1) // LANES * LANES
    projected = widen(
        jnp.concatenate(
            [
                jnp.dot(normed_ref[...], weight[:, columns], preferred_element_type=jnp.float32)
                for columns in (slice(0, middle), slice(middle, weight.shape[1]))
            ],
            axis=1,
        )
    )
    total = projected.shape[0]
    cosine, sine = cos_ref[...], sin_ref[...]
    live = lax.broadcasted_iota(jnp.int32, (1, total), 1) < scalars[0]
    for g in range(groups):
        for i in range(GROUP + 2):
            head = window_at(projected, (g * (GROUP + 2) + i) * HEAD_DIM)
            if i <= GROUP:
                swapped = jnp.where(
                    lane < HEAD_DIM // 2,
                    pltpu.roll(head, LANES - HEAD_DIM // 2, 1),
                    pltpu.roll(head, HEAD_DIM // 2, 1),
                )
                head = head * cosine + swapped * sine
            if i < GROUP:
                query_ref[g * GROUP + i] = head.astype(jnp.bfloat16)
            else:
                turned = jnp.transpose(head)[:HEAD_DIM, :]
                first = (2 * g + i - GROUP) * HEAD_DIM
                rows = slice(first, first + HEAD_DIM)
                new_ref[rows, :] = turned.astype(jnp.bfloat16)
                written_ref[rows, :] = jnp.where(live, turned, 0.0).astype(jnp.bfloat16)


def project(scalars, first_piece, normed, cosine, sine, pieces):
    total, width = normed.shape
    columns = pieces[0].shape[1]
    groups = columns // ((GROUP + 2) * HEAD_DIM)
    count = len(pieces)
    return kernel_call(
        functools.partial(project_kernel, count, first_piece, groups),
        "project",
        32,
        8,
        grid_spec=pltpu.PrefetchScalarGridSpec(
            num_scalar_prefetch=1,
            grid=(),
            in_specs=[WHOLE] * 3 + [ANYWHERE] * count,
            out_specs=[WHOLE] * 4,
            scratch_shapes=[
                pltpu.VMEM((width, columns), jnp.bfloat16),
                pltpu.SemaphoreType.DMA((count,)),
            ],
        ),
        out_shape=[
            jax.ShapeDtypeStruct((groups * GROUP, total, LANES), jnp.bfloat16),
            jax.ShapeDtypeStruct((groups * 2 * HEAD_DIM, total), jnp.bfloat16),
            jax.ShapeDtypeStruct((groups * 2 * HEAD_DIM, total), jnp.bfloat16),
            MARK,
        ],
    )(scalars, normed, cosine, sine, *pieces)


def attend_kernel(extras, group, begin_chunk, count, chunk, scalars, *refs):
    query_ref, cache_ref, new_ref = refs[:3]
    out_ref = refs[3 + extras]
    keys, values, sems = refs[4 + extras :]
    length, prefix = scalars[0], scalars[1]
    rows = GROUP * chunk
    oldest = WINDOW - prefix
    lane = lax.broadcasted_iota(jnp.int32, (1, VALUE_ROWS), 1)
    factor = SCORE_SCALE * LOG2E
    offset = group * GROUP * HEAD_DIM % LANES
    total_slots = keys.shape[1]
    span = (chunk + LANES - 1) // LANES * LANES
    head_rows = pl.ds(0, HEAD_DIM)
    spans = [(WINDOW, total_slots - WINDOW)] + [(i, KEY_TILE) for i in range(0, WINDOW, KEY_TILE)]
    copies = []
    for n, (start, size) in enumerate(spans):
        for k, room in enumerate((keys, values)):
            if n == 0:
                source = new_ref.at[pl.ds((2 * group + k) * HEAD_DIM, HEAD_DIM), :]
            else:
                source = cache_ref.at[pl.ds((2 * group + k) * HEAD_DIM, HEAD_DIM), pl.ds(start, size)]
            copies.append(
                pltpu.make_async_copy(source, room.at[head_rows, pl.ds(start, size)], sems.at[2 * n + k])
            )
            copies[-1].start()
    ones = lax.broadcasted_iota(jnp.int32, (VALUE_ROWS - HEAD_DIM, total_slots), 0) == 0
    values[HEAD_DIM:, :] = ones.astype(jnp.float32).astype(jnp.bfloat16)
    for copy in copies[:2]:
        copy.wait()
    for copy in copies[2:]:
        copy.wait()

    def one_chunk(j, unused):
        first = pl.multiple_of(scalars[2 + begin_chunk + j], 16)
        base = pl.multiple_of(first // LANES * LANES, LANES)
        here = pl.ds(pl.multiple_of(j * chunk, 16), chunk)

        @pl.when(first >= length)
        def _():
            out_ref[here, :] = jnp.zeros((chunk, GROUP_OUT), jnp.bfloat16)

        @pl.when(first < length)
        def _():
            query = query_ref[:, pl.ds(first, chunk), :].reshape(rows, LANES)[:, :HEAD_DIM]
            token = lax.broadcasted_iota(jnp.int32, (GROUP, chunk, 1), 1).reshape(rows, 1) + first

            def scores_of(start, size):
                return jnp.dot(query, keys[:, pl.ds(start, size)], preferred_element_type=jnp.float32)

            ahead_of = lax.broadcasted_iota(jnp.int32, (1, span), 1) - (token - base)

            def recent(scores):
                return jnp.where(ahead_of <= 0, scores, -jnp.inf)

            def oldest_in(scores, start):
                slot = lax.broadcasted_iota(jnp.int32, (1, KEY_TILE), 1) + start
                scores = jnp.where(slot >= oldest, scores, -jnp.inf)
                edge = jnp.where(ahead_of + (start - base) > 0, scores[:, :span], -jnp.inf)
                return jnp.concatenate([edge, scores[:, span:]], axis=1)

            def fold(scores, start, size, carry):
                top, total = carry
                new_top = jnp.maximum(top, jnp.max(scores, axis=1, keepdims=True))
                weights = jnp.exp2((scores - new_top) * factor).astype(jnp.bfloat16)
                shrink = jnp.exp2((top - new_top) * factor)
                added = lax.dot_general(
                    weights,
                    values[:, pl.ds(start, size)],
                    (((1,), (1,)), ((), ())),
                    preferred_element_type=jnp.float32,
                )
                return new_top, total * shrink + added

            def finish(total):
                result = total / total[:, HEAD_DIM : HEAD_DIM + 1]
                result = jnp.where((token < length) & (lane < HEAD_DIM), result, 0.0)
                rest = jnp.zeros((rows, 2 * LANES - VALUE_ROWS), jnp.float32)
                result = jnp.concatenate([result, rest], axis=1).reshape(GROUP, chunk, 2 * LANES)
                columns = [None] * (GROUP_OUT // LANES + 1)
                for i in range(GROUP):
                    start = offset + i * HEAD_DIM
                    base, shift = start // LANES, start % LANES
                    pair = pltpu.roll(result[i], shift, 1) if shift else result[i]
                    for k in range(2):
                        piece = pair[:, k * LANES : (k + 1) * LANES]
                        old = columns[base + k]
                        columns[base + k] = piece if old is None else old + piece
                wide = jnp.concatenate(columns[: GROUP_OUT // LANES], axis=1)
                out_ref[here, :] = wide.astype(jnp.bfloat16)

            def at(i):
                return pl.multiple_of(base + i * KEY_TILE, LANES)

            newest = at(WINDOW // KEY_TILE)
            none = (
                jnp.full((rows, 1), -1e38, jnp.float32),
                jnp.zeros((rows, VALUE_ROWS), jnp.float32),
            )
            begin = jnp.clip((oldest - base) // KEY_TILE, 0, WINDOW // KEY_TILE - 1)

            @pl.when(begin == 0)
            def _():
                scores = recent(scores_of(newest, span))
                start, size, carry = newest, span, none
                for i in range(WINDOW // KEY_TILE):
                    coming = scores_of(at(i), KEY_TILE)
                    if i == 0:
                        coming = oldest_in(coming, at(0))
                    carry = fold(scores, start, size, carry)
                    scores, start, size = coming, at(i), KEY_TILE
                finish(fold(scores, start, size, carry)[1])

            @pl.when(begin > 0)
            def _():
                carry = fold(recent(scores_of(newest, span)), newest, span, none)
                carry = fold(oldest_in(scores_of(at(begin), KEY_TILE), at(begin)), at(begin), KEY_TILE, carry)

                def step(i, c):
                    return fold(scores_of(at(i), KEY_TILE), at(i), KEY_TILE, c)

                finish(lax.fori_loop(begin + 1, WINDOW // KEY_TILE, step, carry)[1])

        return unused

    lax.fori_loop(0, count, one_chunk, 0)


def attend(scalars, query, cache, new, group, half, chunk, extras=()):
    total = query.shape[1]
    rows = total // 2
    count = rows // chunk
    slots = WINDOW + total
    return kernel_call(
        functools.partial(attend_kernel, len(extras), group, half * count, count, chunk),
        "attend",
        32,
        10,
        grid_spec=pltpu.PrefetchScalarGridSpec(
            num_scalar_prefetch=1,
            grid=(1,),
            in_specs=[pl.BlockSpec((GROUP, total, LANES), lambda i, s: (group, 0, 0))]
            + [ANYWHERE] * (2 + len(extras)),
            out_specs=pl.BlockSpec((rows, GROUP_OUT), lambda i, s: (0, 0)),
            scratch_shapes=[
                pltpu.VMEM((HEAD_DIM, slots), jnp.bfloat16),
                pltpu.VMEM((VALUE_ROWS, slots), jnp.bfloat16),
                pltpu.SemaphoreType.DMA((2 * (1 + WINDOW // KEY_TILE),)),
            ],
        ),
        out_shape=jax.ShapeDtypeStruct((rows, GROUP_OUT), jnp.bfloat16),
    )(scalars, query, cache, new, *extras)


def output_kernel(groups, pieces, first_piece, scalars, *refs):
    attended = refs[:groups]
    if pieces:
        parts = refs[groups : groups + pieces]
        out_refs, weight, sems = refs[groups + pieces : -2], refs[-2], refs[-1]
        copies = []
        for i in range(pieces):
            rows = parts[i].shape[0]
            place = pl.multiple_of(scalars[first_piece + i], 16)
            copies.append(
                pltpu.make_async_copy(parts[i], weight.at[pl.ds(place, rows), :], sems.at[i])
            )
            copies[-1].start()
        for copy in copies:
            copy.wait()
    else:
        weight, out_refs = refs[groups], refs[groups + 1 :]
    depth = weight.shape[1]
    columns = [None] * (depth // LANES + 1)
    for g in range(groups):
        base = g * GROUP * HEAD_DIM // LANES
        for k in range(GROUP_OUT // LANES):
            piece = attended[g][:, k * LANES : (k + 1) * LANES]
            old = columns[base + k]
            columns[base + k] = piece if old is None else old + piece
    used = (depth + LANES - 1) // LANES
    left = jnp.concatenate(columns[:used], axis=1)[:, :depth]
    product = lax.dot_general(
        left, weight[...], (((1,), (1,)), ((), ())), preferred_element_type=jnp.float32
    )
    row = 0
    for out in out_refs:
        out[...] = product[row : row + out.shape[0], :].astype(out.dtype)
        row += out.shape[0]


def output_products(scalars, first_piece, attended, pieces, outs):
    count = len(pieces) if len(pieces) > 1 else 0
    rows = attended[0].shape[0]
    depth = pieces[0].shape[1]
    width = sum(p.shape[0] for p in pieces)
    made = [(width, depth, jnp.bfloat16)] if count else []
    made = [(r, width, kind) for r, kind in outs] + made
    results = kernel_call(
        functools.partial(output_kernel, len(attended), count, first_piece),
        "output",
        28,
        4.5,
        grid_spec=pltpu.PrefetchScalarGridSpec(
            num_scalar_prefetch=1,
            grid=(),
            in_specs=[WHOLE] * len(attended) + ([ANYWHERE] * count or [WHOLE]),
            out_specs=[WHOLE] * len(made),
            scratch_shapes=[pltpu.SemaphoreType.DMA((count,))] if count else [],
        ),
        out_shape=[jax.ShapeDtypeStruct((r, c), kind) for r, c, kind in made],
    )(scalars, *attended, *pieces)
    return results if count else [*results, pieces[0]]


def rotation_tables(position):
    halfway = HEAD_DIM // 2
    frequency = jnp.exp(
        jnp.arange(halfway, dtype=jnp.float32) * (-2.0 * math.log(10000.0) / HEAD_DIM)
    )
    angles = position.astype(jnp.float32)[..., None] * frequency
    cosine, sine = jnp.cos(angles), jnp.sin(angles)
    rest = jnp.zeros((position.shape[0], LANES - HEAD_DIM), jnp.float32)
    return (
        jnp.concatenate([cosine, cosine, rest], axis=1),
        jnp.concatenate([-sine, sine, rest], axis=1),
    )


def shards(hidden, norm_gain, w_qkv, w_out, kv_cache, new_len, prefix_len):
    seq_index = lax.axis_index("seq")
    head_index = lax.axis_index("head")
    seq_count = lax.axis_size("seq")
    head_count = lax.axis_size("head")
    unused_lead, chunk, width = hidden.shape
    depth, total_cols = w_qkv.shape
    groups = total_cols // ((GROUP + 2) * HEAD_DIM) // head_count
    group_width = (GROUP + 2) * HEAD_DIM
    head_cols = groups * GROUP * HEAD_DIM
    out_depth = w_out.shape[1]
    new_total = head_count * chunk
    paired = head_count == 4
    core_pairs = [(i, i ^ 1) for i in range(head_count)]
    y_pairs = [(i, i ^ 2) for i in range(head_count)]

    if paired:
        order = np.array([[h ^ j for j in range(head_count)] for h in range(head_count)])
    else:
        order = np.array([[(h + j) % head_count for j in range(head_count)] for h in range(head_count)])
    ring_table = np.concatenate([ring_starts(seq_count, depth), ring_starts(seq_count, out_depth)], axis=1)
    place_table = np.concatenate(
        [
            np.zeros((seq_count * head_count, 2), np.int32),
            np.tile((order * chunk).astype(np.int32), (seq_count, 1)),
            np.repeat(ring_table, head_count, axis=0),
        ],
        axis=1,
    )
    places = lax.dynamic_index_in_dim(
        jnp.asarray(place_table), seq_index * head_count + head_index, 0, keepdims=False
    )
    length = lax.dynamic_index_in_dim(new_len, seq_index, 0)
    prefix = lax.dynamic_index_in_dim(prefix_len, seq_index, 0)
    scalars = jnp.concatenate([length, prefix, places[2:]])
    first_qkv = 2 + head_count
    first_out = first_qkv + seq_count

    own_hidden = hidden.reshape(chunk, width)
    if paired:
        far = lax.ppermute(own_hidden, "head", y_pairs)
        last = lax.ppermute(far, "head", core_pairs)
    else:
        gathered = lax.all_gather(own_hidden, "head", axis=0)
        chunks = [
            lax.dynamic_index_in_dim(gathered, (head_index + j) % head_count, 0, keepdims=False)
            for j in range(head_count)
        ]
        far = last = gathered

    ahead, back = ring_pairs(seq_count)
    own_cols = lax.dynamic_slice_in_dim(
        w_qkv, head_index * groups * group_width, groups * group_width, 1
    )
    pieces = [own_cols]
    f = b = own_cols
    cosine, sine = rotation_tables(prefix[0] + jnp.arange(new_total, dtype=jnp.int32))
    final = seq_count // 2
    count = head_count // 2
    for step in range(1, final + 1):
        if step == 2:
            if paired:
                chunks = [own_hidden, lax.ppermute(tie(own_hidden, f), "head", core_pairs), far, last]
            normed, mark = normalize_some(places, 0, chunks[:count], norm_gain, new_total)
        elif step == final - 1:
            f, b = lax.optimization_barrier((f, b, far, mark))[:2]
        elif step == final:
            normed, mark = normalize_some(
                places, count, chunks[count:], norm_gain, new_total, normed
            )
            third = (f, b)
        f = lax.ppermute(f, "seq", ahead)
        if step < final:
            b = lax.ppermute(b, "seq", back)
        pieces += [f, b] if step < final else [f]

    cache = kv_cache.reshape(WINDOW, kv_cache.shape[-1]).T

    out_rows = lax.dynamic_slice_in_dim(w_out, head_index * head_cols, head_cols, 0).T
    out_rows = tie(out_rows, *third)
    attended = [[None] * groups, [None] * groups]
    out_pieces = [out_rows]
    ready = pieces[-1]
    f = b = out_rows
    for step in range(1, final + 1):
        moved = []
        if step > 1:
            f, b = lax.optimization_barrier((f, b, ready))[:2]
            f = lax.ppermute(f, "seq", ahead)
            moved.append(f)
        b = lax.ppermute(b, "seq", back)
        moved.append(b)
        out_pieces += moved
        here = tie(scalars, *moved)
        if step == 1:
            query, new, written, projected = project(here, first_qkv, normed, cosine, sine, pieces)
        elif step == 2:
            ready = projected
        if 1 < step < 2 + groups:
            attended[1][step - 2] = attend(here, query, cache, new, step - 2, 1, chunk)
        if 2 < step < 3 + groups:
            ready = attended[1][step - 3]
    out_pieces = (
        out_pieces[:1]
        + [p for k in range(1, final) for p in (out_pieces[2 * k], out_pieces[2 * k - 1])]
        + out_pieces[-1:]
    )
    for g in range(groups):
        if attended[1][g] is None:
            attended[1][g] = attend(scalars, query, cache, new, g, 1, chunk)
    late = scalars
    arrived = []
    for g in range(groups):
        if paired and g == 0:
            forth, across, whole_weight = output_products(
                scalars, first_out, attended[1], out_pieces, [(chunk, jnp.bfloat16)] * 2
            )
            beside = lax.ppermute(across, "head", core_pairs)
            both = (forth.astype(jnp.float32) + beside.astype(jnp.float32)).astype(jnp.bfloat16)
            cut = (width // groups + LANES - 1) // LANES * LANES
            parts = [both[:, k * cut : (k + 1) * cut] for k in range(groups)]
            late = tie(scalars, *parts)
        attended[0][g] = attend(late, query, cache, new, g, 0, chunk)
        if paired:
            part = tie(parts[g], *attended[0][:g])
            arrived.append(lax.ppermute(part, "head", y_pairs))
            late = tie(late, arrived[g], attended[0][g])
    kv_written = written.T.reshape(1, new_total, groups * 2 * HEAD_DIM)

    if paired:
        own, other, _ = output_products(
            late, first_out, attended[0], [whole_weight], [(chunk, jnp.float32), (chunk, jnp.bfloat16)]
        )
        near = lax.ppermute(other, "head", core_pairs)
        far = jnp.concatenate(arrived, axis=1)
        output = own + near.astype(jnp.float32) + far.astype(jnp.float32)
    else:
        products = [
            output_products(scalars, first_out, part, out_pieces, [(new_total // 2, jnp.bfloat16)])[0]
            for part in attended
        ]
        stacked = jnp.concatenate(products, axis=0).reshape(head_count, chunk, width)
        back = jnp.asarray((np.arange(head_count)[None] - np.arange(head_count)[:, None]) % head_count)
        output = lax.psum_scatter(stacked[back[head_index]], "head", scatter_dimension=0)
    return (output.astype(jnp.bfloat16).reshape(1, chunk, width), kv_written)


def solution(mesh):
    placed = (
        P("seq", "head", None),
        P(),
        P("seq", None),
        P(None, "seq"),
        P("seq", None, "head"),
        P(),
        P(),
    )
    return jax.shard_map(
        shards,
        mesh=mesh,
        in_specs=placed,
        out_specs=(P("seq", "head", None), P("seq", None, "head")),
        check_vma=False,
    )
```

```python
import functools
import math

import jax
import jax.numpy as jnp
import numpy as np
from jax import lax
from jax.experimental import pallas as pl
from jax.experimental.pallas import tpu as pltpu
from jax.sharding import PartitionSpec as P

HEAD_DIM = 80
WINDOW = 4096
GROUP = 4
LANES = 128
KEY_TILE = 1024
VALUE_ROWS = HEAD_DIM + 16
SCORE_SCALE = 1.0 / math.sqrt(HEAD_DIM)
LOG2E = math.log2(math.e)
FLOPS_PER_US = 1.1e9
MARK = jax.ShapeDtypeStruct((8, LANES), jnp.float32)
GROUP_OUT = (GROUP * HEAD_DIM + LANES - 1) // LANES * LANES
WHOLE = pl.BlockSpec(memory_space=pltpu.VMEM)
ANYWHERE = pl.BlockSpec(memory_space=pl.ANY)


def ring_order(count):
    return list(range(0, count, 2)) + list(range(count - 1, 0, -2))


def ring_pairs(count):
    order = ring_order(count)
    ahead = [(order[i], order[(i + 1) % count]) for i in range(count)]
    return ahead, [(b, a) for a, b in ahead]


def ring_starts(count, rows):
    order = ring_order(count)
    place = {owner: i for i, owner in enumerate(order)}
    table = []
    for mine in range(count):
        starts = [mine * rows]
        for step in range(1, count // 2):
            starts.append(order[(place[mine] - step) % count] * rows)
            starts.append(order[(place[mine] + step) % count] * rows)
        opposite = order[(place[mine] + count // 2) % count] * rows
        table.append(starts + [opposite])
    return np.array(table, np.int32)


def kernel_call(body, name, room, micros, **kwargs):
    return pl.pallas_call(
        body,
        compiler_params=pltpu.CompilerParams(vmem_limit_bytes=room * 1024 * 1024),
        cost_estimate=pl.CostEstimate(flops=int(micros * FLOPS_PER_US), bytes_accessed=0, transcendentals=0),
        name=name,
        **kwargs,
    )


def tie(value, *earlier):
    return lax.optimization_barrier((value, *earlier))[0]


def normalize_kernel(count, first_chunk, scalars, *refs):
    chunks, gain_ref = refs[:count], refs[count]
    out_ref, mark_ref, stage, sems = refs[-4:]
    mark_ref[...] = jnp.zeros(mark_ref.shape, jnp.float32)
    copies = []
    for j in range(count):
        rows = chunks[j].shape[0]
        values = chunks[j][...].astype(jnp.float32)
        meansq = jnp.mean(values * values, axis=-1, keepdims=True)
        scaled = values * lax.rsqrt(meansq + 1e-05) * gain_ref[...]
        stage[j] = scaled.astype(jnp.bfloat16)
        place = pl.multiple_of(scalars[2 + first_chunk + j], 16)
        copies.append(pltpu.make_async_copy(stage.at[j], out_ref.at[pl.ds(place, rows), :], sems.at[j]))
        copies[-1].start()
    for copy in copies:
        copy.wait()


def normalize_some(scalars, first_chunk, chunks, gain, total, into=None):
    rows, width = chunks[0].shape
    count = len(chunks)
    more = [] if into is None else [into]
    return kernel_call(
        functools.partial(normalize_kernel, count, first_chunk),
        "normalize",
        16,
        0.05,
        grid_spec=pltpu.PrefetchScalarGridSpec(
            num_scalar_prefetch=1,
            grid=(),
            in_specs=[WHOLE] * (count + 1) + [ANYWHERE] * len(more),
            out_specs=[ANYWHERE, WHOLE],
            scratch_shapes=[
                pltpu.VMEM((count, rows, width), jnp.bfloat16),
                pltpu.SemaphoreType.DMA((count,)),
            ],
        ),
        out_shape=[jax.ShapeDtypeStruct((total, width), jnp.bfloat16), MARK],
        input_output_aliases={count + 2: 0} if more else {},
    )(scalars, *chunks, gain.reshape(1, width), *more)


def window_at(wide, start):
    base = start // LANES * LANES
    if start + HEAD_DIM <= base + LANES:
        view = wide[:, base : base + LANES]
        return view if start == base else pltpu.roll(view, LANES - (start - base), 1)
    view = wide[:, base : base + 2 * LANES]
    return pltpu.roll(view, view.shape[1] - (start - base), 1)[:, :LANES]


def widen(values):
    rows, width = values.shape
    padded = (width + LANES - 1) // LANES * LANES
    if padded == width:
        return values
    return jnp.concatenate([values, jnp.zeros((rows, padded - width), values.dtype)], axis=1)


def project_kernel(pieces, first_piece, groups, scalars, *refs):
    normed_ref, cos_ref, sin_ref = refs[:3]
    parts = refs[3 : 3 + pieces]
    query_ref, new_ref, written_ref, mark_ref = refs[3 + pieces : 7 + pieces]
    weight, part_sems = refs[7 + pieces :]
    mark_ref[...] = jnp.zeros(mark_ref.shape, jnp.float32)
    copies = []
    for i in range(pieces):
        rows = parts[i].shape[0]
        place = pl.multiple_of(scalars[first_piece + i], 16)
        copies.append(
            pltpu.make_async_copy(parts[i], weight.at[pl.ds(place, rows), :], part_sems.at[i])
        )
        copies[-1].start()
    for copy in copies:
        copy.wait()
    lane = lax.broadcasted_iota(jnp.int32, (1, LANES), 1)
    middle = (weight.shape[1] // 2 + LANES - 1) // LANES * LANES
    projected = widen(
        jnp.concatenate(
            [
                jnp.dot(normed_ref[...], weight[:, columns], preferred_element_type=jnp.float32)
                for columns in (slice(0, middle), slice(middle, weight.shape[1]))
            ],
            axis=1,
        )
    )
    total = projected.shape[0]
    cosine, sine = cos_ref[...], sin_ref[...]
    live = lax.broadcasted_iota(jnp.int32, (1, total), 1) < scalars[0]
    for g in range(groups):
        for i in range(GROUP + 2):
            head = window_at(projected, (g * (GROUP + 2) + i) * HEAD_DIM)
            if i <= GROUP:
                swapped = jnp.where(
                    lane < HEAD_DIM // 2,
                    pltpu.roll(head, LANES - HEAD_DIM // 2, 1),
                    pltpu.roll(head, HEAD_DIM // 2, 1),
                )
                head = head * cosine + swapped * sine
            if i < GROUP:
                query_ref[g * GROUP + i] = head.astype(jnp.bfloat16)
            else:
                turned = jnp.transpose(head)[:HEAD_DIM, :]
                first = (2 * g + i - GROUP) * HEAD_DIM
                rows = slice(first, first + HEAD_DIM)
                new_ref[rows, :] = turned.astype(jnp.bfloat16)
                written_ref[rows, :] = jnp.where(live, turned, 0.0).astype(jnp.bfloat16)


def project(scalars, first_piece, normed, cosine, sine, pieces):
    total, width = normed.shape
    columns = pieces[0].shape[1]
    groups = columns // ((GROUP + 2) * HEAD_DIM)
    count = len(pieces)
    return kernel_call(
        functools.partial(project_kernel, count, first_piece, groups),
        "project",
        32,
        8,
        grid_spec=pltpu.PrefetchScalarGridSpec(
            num_scalar_prefetch=1,
            grid=(),
            in_specs=[WHOLE] * 3 + [ANYWHERE] * count,
            out_specs=[WHOLE] * 4,
            scratch_shapes=[
                pltpu.VMEM((width, columns), jnp.bfloat16),
                pltpu.SemaphoreType.DMA((count,)),
            ],
        ),
        out_shape=[
            jax.ShapeDtypeStruct((groups * GROUP, total, LANES), jnp.bfloat16),
            jax.ShapeDtypeStruct((groups * 2 * HEAD_DIM, total), jnp.bfloat16),
            jax.ShapeDtypeStruct((groups * 2 * HEAD_DIM, total), jnp.bfloat16),
            MARK,
        ],
    )(scalars, normed, cosine, sine, *pieces)


def attend_kernel(built, group, begin_chunk, count, chunk, scalars, *refs):
    if built:
        query_ref, keys, values, out_ref = refs
    else:
        query_ref, cache_ref, new_ref, out_ref, keys, values, sems = refs
    length, prefix = scalars[0], scalars[1]
    rows = GROUP * chunk
    oldest = WINDOW - prefix
    lane = lax.broadcasted_iota(jnp.int32, (1, VALUE_ROWS), 1)
    factor = SCORE_SCALE * LOG2E
    offset = group * GROUP * HEAD_DIM % LANES
    total_slots = keys.shape[1]
    span = (chunk + LANES - 1) // LANES * LANES
    head_rows = pl.ds(0, HEAD_DIM)
    if not built:
        spans = [(WINDOW, total_slots - WINDOW)] + [(i, KEY_TILE) for i in range(0, WINDOW, KEY_TILE)]
        copies = []
        for n, (start, size) in enumerate(spans):
            for k, room in enumerate((keys, values)):
                if n == 0:
                    source = new_ref.at[pl.ds((2 * group + k) * HEAD_DIM, HEAD_DIM), :]
                else:
                    source = cache_ref.at[pl.ds((2 * group + k) * HEAD_DIM, HEAD_DIM), pl.ds(start, size)]
                copies.append(
                    pltpu.make_async_copy(source, room.at[head_rows, pl.ds(start, size)], sems.at[2 * n + k])
                )
                copies[-1].start()
        ones = lax.broadcasted_iota(jnp.int32, (VALUE_ROWS - HEAD_DIM, total_slots), 0) == 0
        values[HEAD_DIM:, :] = ones.astype(jnp.float32).astype(jnp.bfloat16)
        for copy in copies[:2]:
            copy.wait()
        for copy in copies[2:]:
            copy.wait()

    def one_chunk(j, unused):
        first = pl.multiple_of(scalars[2 + begin_chunk + j], 16)
        base = pl.multiple_of(first // LANES * LANES, LANES)
        here = pl.ds(pl.multiple_of(j * chunk, 16), chunk)

        @pl.when(first >= length)
        def _():
            out_ref[here, :] = jnp.zeros((chunk, GROUP_OUT), jnp.bfloat16)

        @pl.when(first < length)
        def _():
            query = query_ref[:, pl.ds(first, chunk), :].reshape(rows, LANES)[:, :HEAD_DIM]
            token = lax.broadcasted_iota(jnp.int32, (GROUP, chunk, 1), 1).reshape(rows, 1) + first

            def scores_of(start, size):
                return jnp.dot(query, keys[:, pl.ds(start, size)], preferred_element_type=jnp.float32)

            ahead_of = lax.broadcasted_iota(jnp.int32, (1, span), 1) - (token - base)

            def recent(scores):
                return jnp.where(ahead_of <= 0, scores, -jnp.inf)

            def oldest_in(scores, start):
                slot = lax.broadcasted_iota(jnp.int32, (1, KEY_TILE), 1) + start
                scores = jnp.where(slot >= oldest, scores, -jnp.inf)
                edge = jnp.where(ahead_of + (start - base) > 0, scores[:, :span], -jnp.inf)
                return jnp.concatenate([edge, scores[:, span:]], axis=1)

            def fold(scores, start, size, carry):
                top, total = carry
                new_top = jnp.maximum(top, jnp.max(scores, axis=1, keepdims=True))
                weights = jnp.exp2((scores - new_top) * factor).astype(jnp.bfloat16)
                shrink = jnp.exp2((top - new_top) * factor)
                added = lax.dot_general(
                    weights,
                    values[:, pl.ds(start, size)],
                    (((1,), (1,)), ((), ())),
                    preferred_element_type=jnp.float32,
                )
                return new_top, total * shrink + added

            def finish(total):
                result = total / total[:, HEAD_DIM : HEAD_DIM + 1]
                result = jnp.where((token < length) & (lane < HEAD_DIM), result, 0.0)
                rest = jnp.zeros((rows, 2 * LANES - VALUE_ROWS), jnp.float32)
                result = jnp.concatenate([result, rest], axis=1).reshape(GROUP, chunk, 2 * LANES)
                columns = [None] * (GROUP_OUT // LANES + 1)
                for i in range(GROUP):
                    start = offset + i * HEAD_DIM
                    base, shift = start // LANES, start % LANES
                    pair = pltpu.roll(result[i], shift, 1) if shift else result[i]
                    for k in range(2):
                        piece = pair[:, k * LANES : (k + 1) * LANES]
                        old = columns[base + k]
                        columns[base + k] = piece if old is None else old + piece
                wide = jnp.concatenate(columns[: GROUP_OUT // LANES], axis=1)
                out_ref[here, :] = wide.astype(jnp.bfloat16)

            def at(i):
                return pl.multiple_of(base + i * KEY_TILE, LANES)

            newest = at(WINDOW // KEY_TILE)
            none = (
                jnp.full((rows, 1), -1e38, jnp.float32),
                jnp.zeros((rows, VALUE_ROWS), jnp.float32),
            )
            begin = jnp.clip((oldest - base) // KEY_TILE, 0, WINDOW // KEY_TILE - 1)

            @pl.when(begin == 0)
            def _():
                scores = recent(scores_of(newest, span))
                start, size, carry = newest, span, none
                for i in range(WINDOW // KEY_TILE):
                    coming = scores_of(at(i), KEY_TILE)
                    if i == 0:
                        coming = oldest_in(coming, at(0))
                    carry = fold(scores, start, size, carry)
                    scores, start, size = coming, at(i), KEY_TILE
                finish(fold(scores, start, size, carry)[1])

            @pl.when(begin > 0)
            def _():
                carry = fold(recent(scores_of(newest, span)), newest, span, none)
                carry = fold(oldest_in(scores_of(at(begin), KEY_TILE), at(begin)), at(begin), KEY_TILE, carry)

                def step(i, c):
                    return fold(scores_of(at(i), KEY_TILE), at(i), KEY_TILE, c)

                finish(lax.fori_loop(begin + 1, WINDOW // KEY_TILE, step, carry)[1])

        return unused

    lax.fori_loop(0, count, one_chunk, 0)


def attend(scalars, query, cache, new, group, half, chunk, built=()):
    total = query.shape[1]
    rows = total // 2
    count = rows // chunk
    slots = WINDOW + total
    return kernel_call(
        functools.partial(attend_kernel, bool(built), group, half * count, count, chunk),
        "attend",
        32,
        10,
        grid_spec=pltpu.PrefetchScalarGridSpec(
            num_scalar_prefetch=1,
            grid=(1,),
            in_specs=[pl.BlockSpec((GROUP, total, LANES), lambda i, s: (group, 0, 0))]
            + [WHOLE if built else ANYWHERE] * 2,
            out_specs=[pl.BlockSpec((rows, GROUP_OUT), lambda i, s: (0, 0))] + ([] if built else [WHOLE] * 2),
            scratch_shapes=[] if built else [
                pltpu.SemaphoreType.DMA((2 * (1 + WINDOW // KEY_TILE),)),
            ],
        ),
        out_shape=[jax.ShapeDtypeStruct((rows, GROUP_OUT), jnp.bfloat16)]
        + [jax.ShapeDtypeStruct((r, slots), jnp.bfloat16) for r in (() if built else (HEAD_DIM, VALUE_ROWS))],
    )(scalars, query, *(built or (cache, new)))


def output_kernel(groups, pieces, first_piece, scalars, *refs):
    attended = refs[:groups]
    if pieces:
        parts = refs[groups : groups + pieces]
        out_refs, weight, sems = refs[groups + pieces : -2], refs[-2], refs[-1]
        copies = []
        for i in range(pieces):
            rows = parts[i].shape[0]
            place = pl.multiple_of(scalars[first_piece + i], 16)
            copies.append(
                pltpu.make_async_copy(parts[i], weight.at[pl.ds(place, rows), :], sems.at[i])
            )
            copies[-1].start()
        for copy in copies:
            copy.wait()
    else:
        weight, out_refs = refs[groups], refs[groups + 1 :]
    depth = weight.shape[1]
    columns = [None] * (depth // LANES + 1)
    for g in range(groups):
        base = g * GROUP * HEAD_DIM // LANES
        for k in range(GROUP_OUT // LANES):
            piece = attended[g][:, k * LANES : (k + 1) * LANES]
            old = columns[base + k]
            columns[base + k] = piece if old is None else old + piece
    used = (depth + LANES - 1) // LANES
    left = jnp.concatenate(columns[:used], axis=1)[:, :depth]
    product = lax.dot_general(
        left, weight[...], (((1,), (1,)), ((), ())), preferred_element_type=jnp.float32
    )
    row = 0
    for out in out_refs:
        out[...] = product[row : row + out.shape[0], :].astype(out.dtype)
        row += out.shape[0]


def output_products(scalars, first_piece, attended, pieces, outs):
    count = len(pieces) if len(pieces) > 1 else 0
    rows = attended[0].shape[0]
    depth = pieces[0].shape[1]
    width = sum(p.shape[0] for p in pieces)
    made = [(width, depth, jnp.bfloat16)] if count else []
    made = [(r, width, kind) for r, kind in outs] + made
    results = kernel_call(
        functools.partial(output_kernel, len(attended), count, first_piece),
        "output",
        28,
        4.5,
        grid_spec=pltpu.PrefetchScalarGridSpec(
            num_scalar_prefetch=1,
            grid=(),
            in_specs=[WHOLE] * len(attended) + ([ANYWHERE] * count or [WHOLE]),
            out_specs=[WHOLE] * len(made),
            scratch_shapes=[pltpu.SemaphoreType.DMA((count,))] if count else [],
        ),
        out_shape=[jax.ShapeDtypeStruct((r, c), kind) for r, c, kind in made],
    )(scalars, *attended, *pieces)
    return results if count else [*results, pieces[0]]


def rotation_tables(position):
    halfway = HEAD_DIM // 2
    frequency = jnp.exp(
        jnp.arange(halfway, dtype=jnp.float32) * (-2.0 * math.log(10000.0) / HEAD_DIM)
    )
    angles = position.astype(jnp.float32)[..., None] * frequency
    cosine, sine = jnp.cos(angles), jnp.sin(angles)
    rest = jnp.zeros((position.shape[0], LANES - HEAD_DIM), jnp.float32)
    return (
        jnp.concatenate([cosine, cosine, rest], axis=1),
        jnp.concatenate([-sine, sine, rest], axis=1),
    )


def shards(hidden, norm_gain, w_qkv, w_out, kv_cache, new_len, prefix_len):
    seq_index = lax.axis_index("seq")
    head_index = lax.axis_index("head")
    seq_count = lax.axis_size("seq")
    head_count = lax.axis_size("head")
    unused_lead, chunk, width = hidden.shape
    depth, total_cols = w_qkv.shape
    groups = total_cols // ((GROUP + 2) * HEAD_DIM) // head_count
    group_width = (GROUP + 2) * HEAD_DIM
    head_cols = groups * GROUP * HEAD_DIM
    out_depth = w_out.shape[1]
    new_total = head_count * chunk
    paired = head_count == 4
    core_pairs = [(i, i ^ 1) for i in range(head_count)]
    y_pairs = [(i, i ^ 2) for i in range(head_count)]

    if paired:
        order = np.array([[h ^ j for j in range(head_count)] for h in range(head_count)])
    else:
        order = np.array([[(h + j) % head_count for j in range(head_count)] for h in range(head_count)])
    ring_table = np.concatenate([ring_starts(seq_count, depth), ring_starts(seq_count, out_depth)], axis=1)
    place_table = np.concatenate(
        [
            np.zeros((seq_count * head_count, 2), np.int32),
            np.tile((order * chunk).astype(np.int32), (seq_count, 1)),
            np.repeat(ring_table, head_count, axis=0),
        ],
        axis=1,
    )
    places = lax.dynamic_index_in_dim(
        jnp.asarray(place_table), seq_index * head_count + head_index, 0, keepdims=False
    )
    length = lax.dynamic_index_in_dim(new_len, seq_index, 0)
    prefix = lax.dynamic_index_in_dim(prefix_len, seq_index, 0)
    scalars = jnp.concatenate([length, prefix, places[2:]])
    first_qkv = 2 + head_count
    first_out = first_qkv + seq_count

    own_hidden = hidden.reshape(chunk, width)
    if paired:
        far = lax.ppermute(own_hidden, "head", y_pairs)
        last = lax.ppermute(far, "head", core_pairs)
    else:
        gathered = lax.all_gather(own_hidden, "head", axis=0)
        chunks = [
            lax.dynamic_index_in_dim(gathered, (head_index + j) % head_count, 0, keepdims=False)
            for j in range(head_count)
        ]
        far = last = gathered

    ahead, back = ring_pairs(seq_count)
    own_cols = lax.dynamic_slice_in_dim(
        w_qkv, head_index * groups * group_width, groups * group_width, 1
    )
    pieces = [own_cols]
    f = b = own_cols
    cosine, sine = rotation_tables(prefix[0] + jnp.arange(new_total, dtype=jnp.int32))
    final = seq_count // 2
    count = head_count // 2
    for step in range(1, final + 1):
        if step == 2:
            if paired:
                chunks = [own_hidden, lax.ppermute(tie(own_hidden, f), "head", core_pairs), far, last]
            normed, mark = normalize_some(places, 0, chunks[:count], norm_gain, new_total)
        elif step == final - 1:
            f, b = lax.optimization_barrier((f, b, far, mark))[:2]
        elif step == final:
            normed, mark = normalize_some(
                places, count, chunks[count:], norm_gain, new_total, normed
            )
            third = (f, b)
        f = lax.ppermute(f, "seq", ahead)
        if step < final:
            b = lax.ppermute(b, "seq", back)
        pieces += [f, b] if step < final else [f]

    cache = kv_cache.reshape(WINDOW, kv_cache.shape[-1]).T

    out_rows = lax.dynamic_slice_in_dim(w_out, head_index * head_cols, head_cols, 0).T
    out_rows = tie(out_rows, *third)
    attended = [[None] * groups, [None] * groups]
    laid = [None] * groups
    out_pieces = [out_rows]
    ready = pieces[-1]
    f = b = out_rows
    for step in range(1, final + 1):
        moved = []
        if step > 1:
            f, b = lax.optimization_barrier((f, b, ready))[:2]
            f = lax.ppermute(f, "seq", ahead)
            moved.append(f)
        b = lax.ppermute(b, "seq", back)
        moved.append(b)
        out_pieces += moved
        here = tie(scalars, *moved)
        if step == 1:
            query, new, written, projected = project(here, first_qkv, normed, cosine, sine, pieces)
        elif step == 2:
            ready = projected
        if 1 < step < 2 + groups:
            attended[1][step - 2], *laid[step - 2] = attend(here, query, cache, new, step - 2, 1, chunk)
        if 2 < step < 3 + groups:
            ready = attended[1][step - 3]
    out_pieces = (
        out_pieces[:1]
        + [p for k in range(1, final) for p in (out_pieces[2 * k], out_pieces[2 * k - 1])]
        + out_pieces[-1:]
    )
    for g in range(groups):
        if attended[1][g] is None:
            attended[1][g], *laid[g] = attend(scalars, query, cache, new, g, 1, chunk)
    late = scalars
    arrived = []
    for g in range(groups):
        if paired and g == 0:
            forth, across, whole_weight = output_products(
                scalars, first_out, attended[1], out_pieces, [(chunk, jnp.bfloat16)] * 2
            )
            beside = lax.ppermute(across, "head", core_pairs)
            both = (forth.astype(jnp.float32) + beside.astype(jnp.float32)).astype(jnp.bfloat16)
            cut = (width // groups + LANES - 1) // LANES * LANES
            parts = [both[:, k * cut : (k + 1) * cut] for k in range(groups)]
            late = tie(scalars, *parts)
        (attended[0][g],) = attend(late, query, cache, new, g, 0, chunk, laid[g])
        if paired:
            part = tie(parts[g], *attended[0][:g])
            arrived.append(lax.ppermute(part, "head", y_pairs))
            late = tie(late, arrived[g], attended[0][g])
    kv_written = written.T.reshape(1, new_total, groups * 2 * HEAD_DIM)

    if paired:
        own, other, _ = output_products(
            late, first_out, attended[0], [whole_weight], [(chunk, jnp.float32), (chunk, jnp.bfloat16)]
        )
        near = lax.ppermute(other, "head", core_pairs)
        far = jnp.concatenate(arrived, axis=1)
        output = own + near.astype(jnp.float32) + far.astype(jnp.float32)
    else:
        products = [
            output_products(scalars, first_out, part, out_pieces, [(new_total // 2, jnp.bfloat16)])[0]
            for part in attended
        ]
        stacked = jnp.concatenate(products, axis=0).reshape(head_count, chunk, width)
        back = jnp.asarray((np.arange(head_count)[None] - np.arange(head_count)[:, None]) % head_count)
        output = lax.psum_scatter(stacked[back[head_index]], "head", scatter_dimension=0)
    return (output.astype(jnp.bfloat16).reshape(1, chunk, width), kv_written)


def solution(mesh):
    placed = (
        P("seq", "head", None),
        P(),
        P("seq", None),
        P(None, "seq"),
        P("seq", None, "head"),
        P(),
        P(),
    )
    return jax.shard_map(
        shards,
        mesh=mesh,
        in_specs=placed,
        out_specs=(P("seq", "head", None), P("seq", None, "head")),
        check_vma=False,
    )
```
